128 devices in a mesh: blk: 8 (over z_hi, x), grp: 16 (over z_lo, y, core).
Axes of the slice: x: 4, y: 4, z: 4 (z_hi: 2, z_lo: 2; z = z_hi * 2 + z_lo), core: 2. Of those that a mesh axis runs over, the one named last changes fastest.
Arguments:
- image_teacher: bfloat16 [16384, 1024], P('blk'), may hold values from -6 to 6
- text_teacher: bfloat16 [16384, 1024], P(('blk', 'grp')), may hold values from -6 to 6
- image_student: bfloat16 [16384, 512], P('blk'), may hold values from -6 to 6
- text_student: bfloat16 [16384, 512], P(('blk', 'grp')), may hold values from -6 to 6
Outputs:
- row_loss: float32 [16384], P('blk')
- grad_image: bfloat16 [16384, 512], P(('blk', 'grp'))
- grad_text: bfloat16 [16384, 512], P(('blk', 'grp'))
The draws below stay inside these ranges and needn't reach their ends.
All inputs are finite; a program needn't handle non-finite values.
Results may differ from the reference program's by a relative error of at most 0.022.
Values may be sent and summed in bfloat16 or wider, within the bound.
No kernel may reach another device: no remote copies, remote signals or barrier semaphores. Data moves between devices by JAX's collectives and lax.ppermute only.
A program may use at most 128 MiB of HBM per device.

```python
import math
import jax
import jax.numpy as jnp
from jax import lax

DT = 1024
DS = 512
BATCH = 16384
N_BLK = 8


def aligned_pair(key, width, salt, lowest, highest):
    key = jax.random.fold_in(key, salt)
    key_text, key_image, key_sign, key_gap, key_flat = jax.random.split(key, 5)
    texts = jnp.clip(jax.random.normal(key_text, (BATCH, width), jnp.float32), -4.0, 4.0)
    images = jnp.clip(jax.random.normal(key_image, (BATCH, width), jnp.float32), -4.0, 4.0)
    counter = jnp.arange(8, dtype=jnp.int32)
    spacing = max(BATCH // 8, 2)
    offset = counter * 37 % spacing
    picked = counter * spacing + offset
    lonely = counter * spacing + (offset + spacing // 2) % spacing
    partner = (picked * 5 + BATCH // 3) % (BATCH - 1)
    signs = jnp.where(jax.random.uniform(key_sign, (8, width), jnp.float32) > 0.5, 1.0, -1.0)
    flat_signs = jnp.where(jax.random.uniform(key_flat, (8, width), jnp.float32) > 0.5, 1.0, -1.0)
    target = lowest + (highest - lowest) * counter.astype(jnp.float32) / 7.0
    gap = jax.random.uniform(key_gap, (8,), jnp.float32, 1.5, 2.5)
    strength = target / (18.0 * math.sqrt(width))
    changed = min(32, width)
    factor = gap * math.sqrt(width) / (18.0 * strength * changed)
    column = jnp.arange(width, dtype=jnp.int32)
    aligned_text = signs * strength[:, None]
    second_text = aligned_text * jnp.where(column[None, :] < changed, 1.0 - factor[:, None], 1.0)
    texts = texts.at[partner].set(aligned_text)
    texts = texts.at[partner + 1].set(second_text)
    images = images.at[picked].set(6.0 * signs)
    images = images.at[lonely].set(6.0 * flat_signs)
    return (images, texts)


def draw_image_teacher(key, part):
    images, texts = aligned_pair(key, DT, 11, 120.0, 300.0)
    return images.astype(jnp.bfloat16)


def draw_text_teacher(key, part):
    images, texts = aligned_pair(key, DT, 11, 120.0, 300.0)
    return texts.astype(jnp.bfloat16)


def draw_image_student(key, part):
    images, texts = aligned_pair(key, DS, 12, 140.0, 330.0)
    return images.astype(jnp.bfloat16)


def draw_text_student(key, part):
    images, texts = aligned_pair(key, DS, 12, 140.0, 330.0)
    return texts.astype(jnp.bfloat16)


def setup_inputs(seed: int = 0) -> dict:
    keys = jax.random.split(jax.random.key(seed), 5)
    image_teacher = draw_image_teacher(jax.random.fold_in(keys[4], 71), 0)
    text_teacher = draw_text_teacher(jax.random.fold_in(keys[4], 71), 0)
    image_student = draw_image_student(jax.random.fold_in(keys[4], 71), 0)
    text_student = draw_text_student(jax.random.fold_in(keys[4], 71), 0)
    return dict(image_teacher=image_teacher, text_teacher=text_teacher, image_student=image_student, text_student=text_student)


def reference(image_teacher, text_teacher, image_student, text_student):
    teacher_scale = 3.0 / math.sqrt(DT)
    student_scale = 3.0 / math.sqrt(DS)
    row_count = BATCH // N_BLK

    def row_block(index):
        begin = index * row_count
        left_t = lax.dynamic_slice_in_dim(image_teacher, begin, row_count, 0)
        left_s = lax.dynamic_slice_in_dim(image_student, begin, row_count, 0)
        teacher_logits = jnp.dot(left_t, text_teacher.T, preferred_element_type=jnp.float32) * teacher_scale
        student_logits = jnp.dot(left_s, text_student.T, preferred_element_type=jnp.float32) * student_scale
        lse_t = jax.nn.logsumexp(teacher_logits, axis=1)
        lse_s = jax.nn.logsumexp(student_logits, axis=1)
        prob_t = jnp.exp(teacher_logits - lse_t[:, None])
        prob_s = jnp.exp(student_logits - lse_s[:, None])
        losses = lax.optimization_barrier(jnp.sum(prob_t * (teacher_logits - student_logits), axis=1)) - lse_t + lse_s
        delta = ((prob_s - prob_t) * student_scale).astype(jnp.bfloat16)
        image_part = jnp.dot(delta, text_student, preferred_element_type=jnp.float32).astype(jnp.bfloat16)
        text_part = jnp.dot(delta.T, left_s, preferred_element_type=jnp.float32).astype(jnp.bfloat16)
        return (losses, image_part, text_part)
    losses, image_parts, text_parts = lax.map(row_block, jnp.arange(N_BLK, dtype=jnp.int32))

    def accumulate(total, part):
        return (total + part.astype(jnp.float32), None)
    text_total, unused = lax.scan(accumulate, jnp.zeros((BATCH, DS), jnp.float32), text_parts)
    row_loss = losses.reshape(BATCH)
    grad_image = image_parts.reshape(BATCH, DS)
    return (row_loss, grad_image, text_total.astype(jnp.bfloat16))
```

```python
import functools
import math

import jax
import jax.numpy as jnp
from jax import lax
from jax.experimental import pallas as pl
from jax.experimental.pallas import tpu as pltpu
from jax.sharding import PartitionSpec as P

AXES = ("blk", "grp")
LOG2E = 1.0 / math.log(2.0)
LN2 = math.log(2.0)
VMEM_LIMIT = 32 * 1024 * 1024
F32 = jnp.float32
BF16 = jnp.bfloat16


def place(i):
    b, g = divmod(i, 16)
    zh, x = divmod(b, 4)
    zl, r = divmod(g, 8)
    y, c = divmod(r, 2)
    return zh, x, zl, y, c


def index(zh, x, zl, y, c):
    return (zh * 4 + x) * 16 + (zl * 4 + y) * 2 + c


def permute(v, move):
    return lax.ppermute(v, AXES, [(i, index(*move(*place(i)))) for i in range(128)])


def along_x(k):
    return lambda zh, x, zl, y, c: (zh, (x + k) % 4, zl, y, c)


def along_y(k, flip=0):
    return lambda zh, x, zl, y, c: (zh, x, zl ^ flip, (y + k) % 4, c)


def other_core(zh, x, zl, y, c):
    return (zh, x, zl, y, 1 - c)


def cross_z(zh, x, zl, y, c):
    return (1 - zh, x, 1 - zl, y, c)


NT = (((1,), (1,)), ((), ()))


def logits_kernel(n_text, first, last, scale_t, scale_s, *refs):
    texts = refs[:n_text]
    image_t, image_s = refs[n_text], refs[n_text + 1]
    k = n_text + 2
    before = None
    if not first:
        before = refs[k]
        k += 1
    out_t, out_s, stats = refs[k], refs[k + 1], refs[k + 2]
    width_t = image_t.shape[-1]
    rows_t = image_t[...].reshape(-1, width_t)
    rows_s = image_s[...].reshape(-1, image_s.shape[-1])
    row = 0
    for ref in texts:
        n = ref.shape[0]
        out_t[row : row + n, :] = (
            lax.dot_general(ref[:, :width_t], rows_t, NT, preferred_element_type=F32)
            * scale_t
        )
        out_s[row : row + n, :] = (
            lax.dot_general(ref[:, width_t:], rows_s, NT, preferred_element_type=F32)
            * scale_s
        )
        row += n
    t = out_t[...]
    s = out_s[...]
    top_t = jnp.max(t, axis=0, keepdims=True)
    top_s = jnp.max(s, axis=0, keepdims=True)
    if not first:
        old_t, old_s = before[0:1, :], before[2:3, :]
        top_t = jnp.maximum(top_t, old_t)
        top_s = jnp.maximum(top_s, old_s)
    exp_t = jnp.exp2(t - top_t)
    exp_s = jnp.exp2(s - top_s)
    sum_t = jnp.sum(exp_t, axis=0, keepdims=True)
    sum_s = jnp.sum(exp_s, axis=0, keepdims=True)
    gap = jnp.sum(exp_t * (t - s), axis=0, keepdims=True)
    if not first:
        shrink = jnp.exp2(old_t - top_t)
        sum_t += before[1:2, :] * shrink
        gap += before[4:5, :] * shrink
        sum_s += before[3:4, :] * jnp.exp2(old_s - top_s)
    if last:
        stats[0:1, :] = top_t + jnp.log2(sum_t)
        stats[1:2, :] = top_s + jnp.log2(sum_s)
        stats[2:3, :] = gap / sum_t
        stats[3:4, :] = jnp.zeros_like(gap)
    else:
        stats[0:1, :] = top_t
        stats[1:2, :] = sum_t
        stats[2:3, :] = top_s
        stats[3:4, :] = sum_s
        stats[4:5, :] = gap
        stats[5:8, :] = jnp.zeros((3, gap.shape[1]), F32)


def logits(texts, image_t, image_s, before, last, tile=4):
    blocks, cores, block = image_t.shape[:3]
    rows = blocks * cores * block
    width_t, width_s = image_t.shape[3], image_s.shape[3]
    n = sum(t.shape[0] for t in texts)
    first = before is None
    full = lambda c, j: (0, 0)
    image = lambda c, j: (j, c, 0, 0)
    column = lambda c, j: (0, c * (blocks // tile) + j)
    in_specs = [pl.BlockSpec(t.shape, full) for t in texts]
    in_specs += [
        pl.BlockSpec((tile, None, block, width_t), image),
        pl.BlockSpec((tile, None, block, width_s), image),
    ]
    args = list(texts) + [image_t, image_s]
    if not first:
        in_specs.append(pl.BlockSpec((8, tile * block), column))
        args.append(before)
    depth = 4 if last else 8
    return pl.pallas_call(
        functools.partial(
            logits_kernel,
            len(texts),
            first,
            last,
            3.0 / math.sqrt(width_t) * LOG2E,
            3.0 / math.sqrt(width_s) * LOG2E,
        ),
        grid=(cores, blocks // tile),
        in_specs=in_specs,
        out_specs=[
            pl.BlockSpec((n, tile * block), column),
            pl.BlockSpec((n, tile * block), column),
            pl.BlockSpec((depth, tile * block), column),
        ],
        out_shape=[
            jax.ShapeDtypeStruct((n, rows), F32),
            jax.ShapeDtypeStruct((n, rows), F32),
            jax.ShapeDtypeStruct((depth, rows), F32),
        ],
        compiler_params=pltpu.CompilerParams(vmem_limit_bytes=VMEM_LIMIT),
        cost_estimate=pl.CostEstimate(
            flops=2 * n * rows * (width_t + width_s),
            bytes_accessed=rows * (width_t + width_s) * 2 + 8 * n * rows,
            transcendentals=2 * n * rows,
        ),
    )(*args)


def merge(parts):
    def total(v):
        if len(v) == 4:
            return (v[0] + v[2]) + (v[1] + v[3])
        return v[0] + v[1]

    lse_t, lse_s, gap = ([p[k] for p in parts] for k in range(3))
    top_t, top_s = functools.reduce(jnp.maximum, lse_t), functools.reduce(jnp.maximum, lse_s)
    part_t = [jnp.exp2(v - top_t) for v in lse_t]
    sum_t = total(part_t)
    mean = total([p * g for p, g in zip(part_t, gap)]) / sum_t
    new_s = top_s + jnp.log2(total([jnp.exp2(v - top_s) for v in lse_s]))
    return jnp.stack([top_t + jnp.log2(sum_t), new_s, mean, jnp.zeros_like(mean)])


ORDER = ((0, 0), (1, 0), (1, 1), (2, 1), (1, 2), (2, 2), (2, 0), (3, 0))


def delta_kernel(n_group, n_text, scale, which, *refs):
    logit_t, logit_s = refs[:n_group], refs[n_group : 2 * n_group]
    texts = refs[2 * n_group : 2 * n_group + n_text]
    stats, grad, delta, turned = refs[2 * n_group + n_text :]
    n = texts[0].shape[0]

    @pl.when(pl.program_id(0) == 0)
    def _():
        for k, ref in enumerate(texts):
            turned[:, n * k : n * k + n] = ref[...].T

    lse_t, lse_s = stats[0:1, :], stats[1:2, :]
    for k, (group, at) in enumerate(ORDER):
        prob_t = jnp.exp2(logit_t[group][n * at : n * at + n, :] - lse_t)
        prob_s = jnp.exp2(logit_s[group][n * at : n * at + n, :] - lse_s)
        delta[n * k : n * k + n, :] = ((prob_s - prob_t) * scale).astype(BF16)
    out = jnp.dot(turned[...], delta[...], preferred_element_type=F32).astype(BF16)
    for k in range(grad.shape[0]):
        grad[k, :, :] = out[:, 128 * k : 128 * k + 128]


def delta_part(half, groups_t, groups_s, texts, stats, width_s, tile=256):
    rows = stats.shape[1]
    count = sum(t.shape[0] for t in texts)
    steps = rows // 2 // tile
    column = lambda i, w: (0, w[0] * steps + i)
    in_specs = [pl.BlockSpec((t.shape[0], tile), column) for t in groups_t + groups_s]
    in_specs += [pl.BlockSpec((t.shape[0], width_s), lambda i, w: (0, 2)) for t in texts]
    in_specs.append(pl.BlockSpec((4, tile), column))
    return pl.pallas_call(
        functools.partial(delta_kernel, len(groups_t), len(texts), 3.0 / math.sqrt(width_s)),
        grid_spec=pltpu.PrefetchScalarGridSpec(
            num_scalar_prefetch=1,
            grid=(steps,),
            in_specs=in_specs,
            out_specs=[
                pl.BlockSpec((tile // 128, width_s, 128), lambda i, w: (i, 0, 0)),
                pl.BlockSpec((count, tile), lambda i, w: (0, i)),
            ],
            scratch_shapes=[pltpu.VMEM((width_s, count), BF16)],
        ),
        out_shape=[
            jax.ShapeDtypeStruct((rows // 256, width_s, 128), BF16),
            jax.ShapeDtypeStruct((count, rows // 2), BF16),
        ],
        compiler_params=pltpu.CompilerParams(vmem_limit_bytes=VMEM_LIMIT),
        cost_estimate=pl.CostEstimate(
            flops=count * rows * width_s,
            bytes_accessed=6 * count * rows,
            transcendentals=count * rows,
        ),
    )(half, *groups_t, *groups_s, *texts, stats)


def text_kernel(half, mine, other, image_mine, image_other, out):
    rows, width = mine.shape[1], out.shape[1]
    out[...] = (
        jnp.dot(mine[...], image_mine[...].reshape(rows, width), preferred_element_type=F32)
        + jnp.dot(other[...], image_other[...].reshape(rows, width), preferred_element_type=F32)
    ).astype(BF16)


def text_part(half, mine, other, image_s, part):
    blocks, _, block, width = image_s.shape
    count, rows = mine.shape
    tile = count // 4
    image = (blocks, None, block, width)
    return pl.pallas_call(
        text_kernel,
        grid_spec=pltpu.PrefetchScalarGridSpec(
            num_scalar_prefetch=1,
            grid=(1,),
            in_specs=[
                pl.BlockSpec((tile, rows), lambda i, w: (part, 0)),
                pl.BlockSpec((tile, rows), lambda i, w: (part, 0)),
                pl.BlockSpec(image, lambda i, w: (0, w[0], 0, 0)),
                pl.BlockSpec(image, lambda i, w: (0, 1 - w[0], 0, 0)),
            ],
            out_specs=pl.BlockSpec((tile, width), lambda i, w: (0, 0)),
        ),
        out_shape=jax.ShapeDtypeStruct((tile, width), BF16),
        compiler_params=pltpu.CompilerParams(vmem_limit_bytes=VMEM_LIMIT),
        cost_estimate=pl.CostEstimate(
            flops=4 * tile * rows * width,
            bytes_accessed=4 * tile * rows + 4 * rows * width,
            transcendentals=0,
        ),
    )(half, mine, other, image_s, image_s)


def pair_kernel(order, mine, other, *outs):
    for k, out in enumerate(outs):
        total = mine[order[k]].astype(F32) + other[order[k]].astype(F32)
        out[...] = total.astype(out.dtype)


def pair_sum(order, mine, other):
    blocks, width, block = mine.shape
    whole = lambda i, w: (0, 0, 0)
    return pl.pallas_call(
        pair_kernel,
        grid_spec=pltpu.PrefetchScalarGridSpec(
            num_scalar_prefetch=1,
            grid=(1,),
            in_specs=[pl.BlockSpec(mine.shape, whole)] * 2,
            out_specs=[pl.BlockSpec((width, block), lambda i, w: (0, 0))] * blocks,
        ),
        out_shape=[
            jax.ShapeDtypeStruct((width, block), F32 if k == 0 else BF16) for k in range(blocks)
        ],
        compiler_params=pltpu.CompilerParams(vmem_limit_bytes=VMEM_LIMIT),
        cost_estimate=pl.CostEstimate(
            flops=blocks * width * block, bytes_accessed=6 * blocks * width * block, transcendentals=0
        ),
    )(order, mine, other)


def total(parts):
    return functools.reduce(jnp.add, [p.astype(F32) for p in parts])


def shards(image_t, text_t, image_s, text_s):
    width_s = image_s.shape[1]
    n = text_t.shape[0]
    image_t = image_t.reshape(8, 2, 128, image_t.shape[1])
    image_s = image_s.reshape(8, 2, 128, width_s)
    own = jnp.concatenate((text_t, text_s), axis=1)

    across = permute(own, cross_z)
    left = permute(own, along_x(1))
    right = permute(own, along_x(3))
    t0, s0, stats = logits([own], image_t, image_s, None, False)
    far = jnp.concatenate(
        (permute(left[: n // 2], along_x(1)), permute(right[n // 2 :], along_x(3))), axis=0
    )
    across_left = permute(across, along_x(1))
    across_right = permute(across, along_x(3))
    t1, s1, stats = logits([across, left, right], image_t, image_s, stats, False)
    across_far = permute(far, cross_z)
    t2, s2, stats = logits([far, across_left, across_right], image_t, image_s, stats, False)
    t3, s3, stats = logits([across_far], image_t, image_s, stats, True)

    stats = merge([stats, permute(stats, other_core)])
    stats = merge([stats, permute(stats, along_y(0, 1))])
    stats = merge([stats] + [permute(stats, along_y(k)) for k in (1, 2, 3)])
    row_loss = (stats[2] - stats[0] + stats[1]) * LN2
    row_loss = row_loss.reshape(2, 8, 128).transpose(1, 0, 2).reshape(-1)

    spot = lax.axis_index("grp")
    core, y, z_lo = lax.rem(spot, 2), lax.rem(spot // 2, 4), spot // 8
    mine = jnp.reshape(core, (1,)).astype(jnp.int32)
    moves = [(0, 0)] + [(2, 1), (2, 0), (1, 1), (3, 1), (1, 0), (3, 0), (0, 1)]
    order = jnp.stack(
        [jnp.bitwise_xor(z_lo, flip) * 4 + lax.rem(y + k, 4) for k, flip in moves]
    ).astype(jnp.int32)
    groups_t, groups_s = (t0, t1, t2, t3), (s0, s1, s2, s3)
    texts = [own, across, left, across_left, right, across_right, far, across_far]
    grad_other, delta_other = delta_part(1 - mine, groups_t, groups_s, texts, stats, width_s)
    received = permute(grad_other, other_core)
    grad_mine, delta_mine = delta_part(mine, groups_t, groups_s, texts, stats, width_s)
    image_terms = pair_sum(order, grad_mine, received)
    image_terms = list(image_terms[:1]) + [
        permute(v, along_y(k, flip)) for v, (k, flip) in zip(image_terms[1:], moves[1:])
    ]
    grad_image = total(image_terms).T.astype(BF16)

    part = lambda k: text_part(mine, delta_mine, delta_other, image_s, k)
    text_terms = [
        permute(part(3), along_x(2)),
        permute(part(1), along_x(3)),
        permute(part(2), along_x(1)),
        part(0),
    ]
    text_sum = total(text_terms)
    from_across = permute(text_sum[n:].astype(BF16), cross_z)
    grad_text = (text_sum[:n] + from_across.astype(F32)).astype(BF16)
    return row_loss, grad_image, grad_text


def solution(mesh):
    in_specs = (P("blk", None), P(AXES, None), P("blk", None), P(AXES, None))
    out_specs = (P("blk"), P(AXES, None), P(AXES, None))
    return jax.shard_map(shards, mesh=mesh, in_specs=in_specs, out_specs=out_specs, check_vma=False)
```

```python
import functools
import math

import jax
import jax.numpy as jnp
from jax import lax
from jax.experimental import pallas as pl
from jax.experimental.pallas import tpu as pltpu
from jax.sharding import PartitionSpec as P

AXES = ("blk", "grp")
LOG2E = 1.0 / math.log(2.0)
LN2 = math.log(2.0)
MIB = 1024 * 1024
F32 = jnp.float32
BF16 = jnp.bfloat16
VMEM = pltpu.VMEM
LANES = 128
WIDE = 256


def place(i):
    b, g = divmod(i, 16)
    zh, x = divmod(b, 4)
    zl, r = divmod(g, 8)
    y, c = divmod(r, 2)
    return zh, x, zl, y, c


def index(zh, x, zl, y, c):
    return (zh * 4 + x) * 16 + (zl * 4 + y) * 2 + c


def permute(v, move):
    return lax.ppermute(v, AXES, [(i, index(*move(*place(i)))) for i in range(128)])


def along_x(k):
    return lambda zh, x, zl, y, c: (zh, (x + k) % 4, zl, y, c)


def along_y(k, flip=0):
    return lambda zh, x, zl, y, c: (zh, x, zl ^ flip, (y + k) % 4, c)


def other_core(zh, x, zl, y, c):
    return (zh, x, zl, y, 1 - c)


def other_core_and_z(zh, x, zl, y, c):
    return (zh, x, 1 - zl, y, 1 - c)


def cross_z(zh, x, zl, y, c):
    return (1 - zh, x, 1 - zl, y, c)


def call(body, args, out_shape, limit, flops=0, size=0, exps=0, **more):
    specs = [pl.BlockSpec(memory_space=space) for space, _ in args]
    values = [
        v if space is pltpu.SMEM else pltpu.with_memory_space_constraint(v, space)
        for space, v in args
    ]
    return pl.pallas_call(
        body,
        in_specs=specs,
        out_specs=[pl.BlockSpec(memory_space=VMEM)] * len(out_shape),
        out_shape=[VMEM(*s) for s in out_shape],
        compiler_params=pltpu.CompilerParams(vmem_limit_bytes=limit * MIB),
        cost_estimate=pl.CostEstimate(flops=flops, bytes_accessed=size, transcendentals=exps),
        **more,
    )(*values)


def join_kernel(text_t, text_s, out, sems):
    width = text_t.shape[1]
    copies = [
        pltpu.make_async_copy(text_t, out.at[:, :width], sems.at[0]),
        pltpu.make_async_copy(text_s, out.at[:, width:], sems.at[1]),
    ]
    for copy in copies:
        copy.start()
    for copy in copies:
        copy.wait()


def join(text_t, text_s):
    n, width = text_t.shape[0], text_t.shape[1] + text_s.shape[1]
    return call(
        join_kernel,
        [(pltpu.HBM, text_t), (pltpu.HBM, text_s)],
        [((n, width), BF16)],
        4,
        scratch_shapes=[pltpu.SemaphoreType.DMA((2,))],
    )[0]


def scales(width_t, width_s):
    return 3.0 / math.sqrt(width_t) * LOG2E, 3.0 / math.sqrt(width_s) * LOG2E


def tile_logits(parts, image_t, image_s, logit_t, logit_s, before, cols):
    scale_t, scale_s = scales(image_t.shape[0], image_s.shape[0])
    tops_t, tops_s = [], []
    for at, text_t, text_s in parts:
        n = text_t.shape[0]
        t = jnp.dot(text_t, image_t[:, cols], preferred_element_type=F32) * scale_t
        s = jnp.dot(text_s, image_s[:, cols], preferred_element_type=F32) * scale_s
        logit_t[at : at + n, cols] = t
        logit_s[at : at + n, cols] = s
        tops_t.append(jnp.max(t, axis=0, keepdims=True))
        tops_s.append(jnp.max(s, axis=0, keepdims=True))
    if before is not None:
        old_t, sum_t, old_s, sum_s, gap = (before[k : k + 1, cols] for k in range(5))
        tops_t.append(old_t)
        tops_s.append(old_s)
    top_t = functools.reduce(jnp.maximum, tops_t)
    top_s = functools.reduce(jnp.maximum, tops_s)
    sums = []
    for at, text_t, _ in parts:
        n = text_t.shape[0]
        t = logit_t[at : at + n, cols]
        s = logit_s[at : at + n, cols]
        exp_t = jnp.exp2(t - top_t)
        sums.append(
            [
                jnp.sum(v, axis=0, keepdims=True)
                for v in (exp_t, jnp.exp2(s - top_s), exp_t * (t - s))
            ]
        )
    if before is not None:
        shrink = jnp.exp2(old_t - top_t)
        sums.append([sum_t * shrink, sum_s * jnp.exp2(old_s - top_s), gap * shrink])
    new_t, new_s, new_gap = (functools.reduce(jnp.add, v) for v in zip(*sums))
    return top_t, new_t, top_s, new_s, new_gap


def put_running(stats, cols, values):
    for k, v in enumerate(values):
        stats[k : k + 1, cols] = v
    stats[5:8, cols] = jnp.zeros((3, values[0].shape[1]), F32)


def first_kernel(
    own, far_t, far_s, image_t, image_s, logit_t, logit_s, turned, stats, held_t, held_s, sems
):
    blocks, cores, block, width_t = far_t.shape
    width_s = far_s.shape[3]
    half = blocks // 2
    wide = half * block
    copies = []
    for k in range(2 * cores):
        c, j = divmod(k, 2)
        pieces = [
            pltpu.make_async_copy(far_t.at[half * j : half * j + half, c], held_t.at[k], sems.at[k, 0]),
            pltpu.make_async_copy(far_s.at[half * j : half * j + half, c], held_s.at[k], sems.at[k, 1]),
        ]
        for piece in pieces:
            piece.start()
        copies.append(pieces)
    turned[:, : own.shape[0]] = own[:, width_t:].T
    for k, pieces in enumerate(copies):
        for piece in pieces:
            piece.wait()
        cols = slice(k * wide, k * wide + wide)
        image_t[:, cols] = held_t[k].reshape(wide, width_t).T
        image_s[:, cols] = held_s[k].reshape(wide, width_s).T
        parts = [(0, own[:, :width_t], own[:, width_t:])]
        for at in range(k * wide, k * wide + wide, WIDE):
            cols = slice(at, at + WIDE)
            put_running(
                stats, cols, tile_logits(parts, image_t, image_s, logit_t, logit_s, None, cols)
            )


def first_logits(own, image_t, image_s, texts):
    blocks, cores, block, width_t = image_t.shape
    width_s = image_s.shape[3]
    rows = blocks * cores * block
    out = [
        ((width_t, rows), BF16),
        ((width_s, rows), BF16),
        ((texts, rows), F32),
        ((texts, rows), F32),
        ((width_s, texts), BF16),
        ((8, rows), F32),
    ]
    n = own.shape[0]
    return call(
        first_kernel,
        [(VMEM, own), (pltpu.HBM, image_t), (pltpu.HBM, image_s)],
        out,
        12,
        flops=2 * n * rows * (width_t + width_s),
        size=2 * rows * (width_t + width_s),
        exps=2 * n * rows,
        scratch_shapes=[
            pltpu.VMEM((2 * cores, blocks // 2, block, width_t), BF16),
            pltpu.VMEM((2 * cores, blocks // 2, block, width_s), BF16),
            pltpu.SemaphoreType.DMA((2 * cores, 2)),
        ],
    )


def more_kernel(places, last, *refs):
    count = len(places)
    texts = refs[:count]
    image_t, image_s, _, _, _, before, logit_t, logit_s, turned, stats = refs[count:]
    width_t, rows = image_t.shape
    for at, ref in zip(places, texts):
        turned[:, at : at + ref.shape[0]] = ref[:, width_t:].T
    for begin in range(0, rows, WIDE):
        cols = slice(begin, begin + WIDE)
        parts = [(at, ref[:, :width_t], ref[:, width_t:]) for at, ref in zip(places, texts)]
        top_t, sum_t, top_s, sum_s, gap = values = tile_logits(
            parts, image_t, image_s, logit_t, logit_s, before, cols
        )
        if not last:
            put_running(stats, cols, values)
            continue
        found = (top_t + jnp.log2(sum_t), top_s + jnp.log2(sum_s), gap / sum_t)
        for q, v in enumerate(found):
            for j in range(WIDE // LANES):
                row = q * (rows // LANES) + begin // LANES + j
                stats[row : row + 1, :] = v[:, j * LANES : j * LANES + LANES]


def more_logits(chunks, state, last=False):
    places = tuple(at for at, _ in chunks)
    image_t, image_s, logit_t, logit_s, turned, stats = state
    width_t, rows = image_t.shape
    width_s = image_s.shape[0]
    n = sum(v.shape[0] for _, v in chunks)
    count = len(chunks)
    shape = ((3 * rows // LANES, LANES), F32) if last else (stats.shape, F32)
    logit_t, logit_s, turned, stats = call(
        functools.partial(more_kernel, places, last),
        [(VMEM, v) for _, v in chunks] + [(VMEM, v) for v in state],
        [(logit_t.shape, F32), (logit_s.shape, F32), (turned.shape, BF16), shape],
        4,
        flops=2 * n * rows * (width_t + width_s),
        size=2 * n * rows,
        exps=2 * n * rows,
        input_output_aliases={count + 2: 0, count + 3: 1, count + 4: 2},
    )
    return image_t, image_s, logit_t, logit_s, turned, stats


def merged(parts):
    def total(v):
        return (v[0] + v[1]) + (v[2] + v[3])

    rows = parts[0].shape[0] // 3
    lse_t, lse_s, gap = ([p[rows * k : rows * k + rows, :] for p in parts] for k in range(3))
    top_t = functools.reduce(jnp.maximum, lse_t)
    top_s = functools.reduce(jnp.maximum, lse_s)
    part_t = [jnp.exp2(v - top_t) for v in lse_t]
    sum_t = total(part_t)
    mean = total([p * g for p, g in zip(part_t, gap)]) / sum_t
    all_s = top_s + jnp.log2(total([jnp.exp2(v - top_s) for v in lse_s]))
    return top_t + jnp.log2(sum_t), all_s, mean


def merge_kernel(a, b, c, d, _, __, out, *held):
    rows = out.shape[0] // 3
    for k, v in enumerate(merged((a, b, c, d))):
        out[rows * k : rows * k + rows, :] = v


def merge(parts, held):
    out, *held = call(
        merge_kernel,
        [(VMEM, v) for v in (*parts, *held)],
        [(parts[0].shape, F32)] + [(v.shape, F32) for v in held],
        4,
        input_output_aliases={4: 1, 5: 2},
    )
    return out, held


def put_merged(parts, lse, loss):
    rows = lse.shape[0] // 2
    all_t, all_s, mean = merged(parts)
    lse[:rows, :] = all_t
    lse[rows:, :] = all_s
    value = (mean - all_t + all_s) * LN2
    for j in range(rows // 2):
        for c in range(2):
            at = c * (rows // 2) + j
            loss[2 * j + c : 2 * j + c + 1, :] = value[at : at + 1, :]


def delta_kernel(scale, logit_t, logit_s, turned, a, b, c, d, grad, delta, loss, lse):
    put_merged((a, b, c, d), lse, loss)
    away = 1 - lax.rem(lax.axis_index("grp"), 2)
    count, rows = logit_t.shape
    half = rows // 2
    pair = WIDE // LANES
    for begin in range(0, rows, WIDE):
        cols = slice(begin, begin + WIDE)
        spots = [begin // LANES + k for k in range(pair)]
        low_t = jnp.concatenate([lse[k : k + 1, :] for k in spots], axis=1)
        low_s = jnp.concatenate(
            [lse[k + rows // LANES : k + rows // LANES + 1, :] for k in spots], axis=1
        )
        prob_t = jnp.exp2(logit_t[:, cols] - low_t)
        prob_s = jnp.exp2(logit_s[:, cols] - low_s)
        delta[begin // half, :, begin % half : begin % half + WIDE] = (
            (prob_s - prob_t) * scale
        ).astype(BF16)
    for begin in range(0, half, WIDE):
        out = jnp.dot(
            turned[...], delta[away, :, begin : begin + WIDE], preferred_element_type=F32
        ).astype(BF16)
        for k in range(pair):
            grad[begin // LANES + k] = out[:, k * LANES : k * LANES + LANES]


def delta_part(logit_t, logit_s, turned, stats):
    count, rows = logit_t.shape
    width = turned.shape[0]
    return call(
        functools.partial(delta_kernel, 3.0 / math.sqrt(width)),
        [(VMEM, v) for v in (logit_t, logit_s, turned, *stats)],
        [
            ((rows // 2 // LANES, width, LANES), BF16),
            ((2, count, rows // 2), BF16),
            ((rows // LANES, LANES), F32),
        ],
        4,
        flops=count * rows * width,
        size=2 * count * rows,
        exps=2 * count * rows,
        scratch_shapes=[pltpu.VMEM((2 * rows // LANES, LANES), F32)],
    )


def text_kernel(delta, image_s, *outs):
    blocks, cores, block, width = image_s.shape
    for k, out in zip((3, 1, 2, 0), outs[1:4] + outs[:1]):
        n = out.shape[0]
        total = 0.0
        for c in range(cores):
            total += jnp.dot(
                delta[c, n * k : n * k + n, :],
                image_s[:, c].reshape(blocks * block, width),
                preferred_element_type=F32,
            )
        out[...] = total.astype(out.dtype)


def text_part(delta, image_s):
    _, count, rows = delta.shape
    width = image_s.shape[3]
    return call(
        text_kernel,
        [(VMEM, delta), (VMEM, image_s)],
        [((count // 4, width), F32 if k == 0 else BF16) for k in range(4)] + [(delta.shape, BF16)],
        6,
        flops=4 * count * rows * width,
        size=count * rows,
        input_output_aliases={0: 4},
    )


def image_kernel(turned, delta, other, *outs):
    spot = lax.axis_index("grp")
    core, y, z = lax.rem(spot, 2), lax.rem(lax.div(spot, 2), 4), lax.div(spot, 8)
    for k, out in zip((2, 1, 3, 0), outs[1:] + outs[:1]):
        for flip in range(2):
            at = (z + flip - 2 * z * flip) * 4 + lax.rem(y + k, 4)
            begin = pl.multiple_of(at * LANES, LANES)
            mine = jnp.dot(
                turned[...], delta[core, :, pl.ds(begin, LANES)], preferred_element_type=F32
            )
            out[flip] = (mine + other[at].astype(F32)).astype(out.dtype)


def image_part(turned, delta, other):
    _, count, rows = delta.shape
    blocks, width, block = other.shape
    return call(
        image_kernel,
        [(VMEM, turned), (VMEM, delta), (VMEM, other)],
        [((2, width, block), F32 if k == 0 else BF16) for k in range(blocks // 2)],
        4,
        flops=2 * count * rows * width,
        size=count * rows,
    )


def total(parts):
    return functools.reduce(jnp.add, [p.astype(F32) for p in parts])


def shards(image_t, text_t, image_s, text_s):
    width_t, width_s = image_t.shape[1], image_s.shape[1]
    n = text_t.shape[0]
    cut = n // 2
    image_t = image_t.reshape(8, 2, 128, width_t)
    image_s = image_s.reshape(8, 2, 128, width_s)

    own = join(text_t, text_s)
    across = permute(own, cross_z)
    left = permute(own, along_x(1))
    right = permute(own, along_x(3))
    state = first_logits(own, image_t, image_s, 8 * n)
    across, left, right, running = lax.optimization_barrier((across, left, right, state[5]))
    state = (*state[:5], running)
    far = jnp.concatenate(
        (permute(left[:cut], along_x(1)), permute(right[cut:], along_x(3))), axis=0
    )
    across_left = permute(across, along_x(1))
    across_right = permute(across, along_x(3))
    across_far = permute(far, cross_z)
    state = more_logits([(n, across), (2 * n, left), (4 * n, right), (6 * n, far)], state)
    state = more_logits([(3 * n, across_left), (5 * n, across_right)], state)
    state = more_logits([(7 * n, across_far)], state, last=True)
    _, _, logit_t, logit_s, turned, stats = state
    stats, (logit_t, logit_s) = merge(
        [stats] + [permute(stats, m) for m in (other_core, along_y(0, 1), other_core_and_z)],
        [logit_t, logit_s],
    )
    stats = [stats] + [permute(stats, along_y(k)) for k in (2, 1, 3)]
    grad_other, delta, row_loss = delta_part(logit_t, logit_s, turned, stats)
    from_core = permute(grad_other, other_core)
    kept_text, *away_text, delta = text_part(delta, image_s)
    kept_image, *away_image = image_part(turned, delta, from_core)
    *away_text, _ = lax.optimization_barrier((*away_text, away_image[0]))
    image_terms = [kept_image] + [permute(v, along_y(k)) for v, k in zip(away_image, (2, 1, 3))]
    text_terms = [kept_text] + [permute(v, along_x(k)) for v, k in zip(away_text, (2, 3, 1))]
    image_sum = total(image_terms)
    from_z = permute(image_sum[1].astype(BF16), along_y(0, 1))
    grad_image = (image_sum[0] + from_z.astype(F32)).T.astype(BF16)
    text_sum = total(text_terms)
    from_across = permute(text_sum[n:].astype(BF16), cross_z)
    grad_text = (text_sum[:n] + from_across.astype(F32)).astype(BF16)
    return row_loss.reshape(-1), grad_image, grad_text


def solution(mesh):
    in_specs = (P("blk", None), P(AXES, None), P("blk", None), P(AXES, None))
    out_specs = (P("blk"), P(AXES, None), P(AXES, None))
    return jax.shard_map(shards, mesh=mesh, in_specs=in_specs, out_specs=out_specs, check_vma=False)
```

```python
import functools
import math

import jax
import jax.numpy as jnp
from jax import lax
from jax.experimental import pallas as pl
from jax.experimental.pallas import tpu as pltpu
from jax.sharding import PartitionSpec as P

AXES = ("blk", "grp")
LOG2E = 1.0 / math.log(2.0)
LN2 = math.log(2.0)
MIB = 1024 * 1024
F32 = jnp.float32
BF16 = jnp.bfloat16
VMEM = pltpu.VMEM
LANES = 128
WIDE = 512


def place(i):
    b, g = divmod(i, 16)
    zh, x = divmod(b, 4)
    zl, r = divmod(g, 8)
    y, c = divmod(r, 2)
    return zh, x, zl, y, c


def index(zh, x, zl, y, c):
    return (zh * 4 + x) * 16 + (zl * 4 + y) * 2 + c


def permute(v, move):
    return lax.ppermute(v, AXES, [(i, index(*move(*place(i)))) for i in range(128)])


def along_x(k):
    return lambda zh, x, zl, y, c: (zh, (x + k) % 4, zl, y, c)


def along_y(k, flip=0):
    return lambda zh, x, zl, y, c: (zh, x, zl ^ flip, (y + k) % 4, c)


def other_core(zh, x, zl, y, c):
    return (zh, x, zl, y, 1 - c)


def other_core_and_z(zh, x, zl, y, c):
    return (zh, x, 1 - zl, y, 1 - c)


def cross_z(zh, x, zl, y, c):
    return (1 - zh, x, 1 - zl, y, c)


def call(body, args, out_shape, limit, flops=0, size=0, exps=0, **more):
    specs = [pl.BlockSpec(memory_space=space) for space, _ in args]
    values = [
        v if space is pltpu.SMEM else pltpu.with_memory_space_constraint(v, space)
        for space, v in args
    ]
    return pl.pallas_call(
        body,
        in_specs=specs,
        out_specs=[pl.BlockSpec(memory_space=VMEM)] * len(out_shape),
        out_shape=[VMEM(*s) for s in out_shape],
        compiler_params=pltpu.CompilerParams(vmem_limit_bytes=limit * MIB),
        cost_estimate=pl.CostEstimate(flops=flops, bytes_accessed=size, transcendentals=exps),
        **more,
    )(*values)


def join_kernel(text_t, text_s, out, sems):
    width = text_t.shape[1]
    copies = [
        pltpu.make_async_copy(text_t, out.at[:, :width], sems.at[0]),
        pltpu.make_async_copy(text_s, out.at[:, width:], sems.at[1]),
    ]
    for copy in copies:
        copy.start()
    for copy in copies:
        copy.wait()


def join(text_t, text_s):
    n, width = text_t.shape[0], text_t.shape[1] + text_s.shape[1]
    return call(
        join_kernel,
        [(pltpu.HBM, text_t), (pltpu.HBM, text_s)],
        [((n, width), BF16)],
        4,
        scratch_shapes=[pltpu.SemaphoreType.DMA((2,))],
    )[0]


def scales(width_t, width_s):
    return 3.0 / math.sqrt(width_t) * LOG2E, 3.0 / math.sqrt(width_s) * LOG2E


def tile_logits(text, spans, image_t, image_s, logit_t, logit_s, before, cols):
    width_t = image_t.shape[0]
    scale_t, scale_s = scales(width_t, image_s.shape[0])
    t = jnp.dot(text[:, :width_t], image_t[:, cols], preferred_element_type=F32) * scale_t
    s = jnp.dot(text[:, width_t:], image_s[:, cols], preferred_element_type=F32) * scale_s
    row = 0
    for at, n in spans:
        logit_t[at : at + n, cols] = t[row : row + n]
        logit_s[at : at + n, cols] = s[row : row + n]
        row += n
    top_t = jnp.max(t, axis=0, keepdims=True)
    top_s = jnp.max(s, axis=0, keepdims=True)
    if before is not None:
        old_t, sum_t, old_s, sum_s, gap = (before[k : k + 1, cols] for k in range(5))
        top_t = jnp.maximum(top_t, old_t)
        top_s = jnp.maximum(top_s, old_s)
    sums = []
    for at, n in spans:
        t = logit_t[at : at + n, cols]
        s = logit_s[at : at + n, cols]
        exp_t = jnp.exp2(t - top_t)
        sums.append(
            [
                jnp.sum(v, axis=0, keepdims=True)
                for v in (exp_t, jnp.exp2(s - top_s), exp_t * (t - s))
            ]
        )
    if before is not None:
        shrink = jnp.exp2(old_t - top_t)
        sums.append([sum_t * shrink, sum_s * jnp.exp2(old_s - top_s), gap * shrink])
    new_t, new_s, new_gap = (functools.reduce(jnp.add, v) for v in zip(*sums))
    return top_t, new_t, top_s, new_s, new_gap


def put_running(stats, cols, values):
    for k, v in enumerate(values):
        stats[k : k + 1, cols] = v
    stats[5:8, cols] = jnp.zeros((3, values[0].shape[1]), F32)


def first_kernel(
    own, far_t, far_s, image_t, image_s, logit_t, logit_s, turned, stats, held_t, held_s, sems
):
    blocks, cores, block, width_t = far_t.shape
    width_s = far_s.shape[3]
    half = blocks // 2
    wide = half * block
    copies = []
    for k in range(2 * cores):
        c, j = divmod(k, 2)
        pieces = [
            pltpu.make_async_copy(far_t.at[half * j : half * j + half, c], held_t.at[k], sems.at[k, 0]),
            pltpu.make_async_copy(far_s.at[half * j : half * j + half, c], held_s.at[k], sems.at[k, 1]),
        ]
        for piece in pieces:
            piece.start()
        copies.append(pieces)
    turned[:, : own.shape[0]] = own[:, width_t:].T
    for k, pieces in enumerate(copies):
        for piece in pieces:
            piece.wait()
        cols = slice(k * wide, k * wide + wide)
        image_t[:, cols] = held_t[k].reshape(wide, width_t).T
        image_s[:, cols] = held_s[k].reshape(wide, width_s).T
        spans = [(0, own.shape[0])]
        put_running(
            stats, cols, tile_logits(own, spans, image_t, image_s, logit_t, logit_s, None, cols)
        )


def first_logits(own, image_t, image_s, texts):
    blocks, cores, block, width_t = image_t.shape
    width_s = image_s.shape[3]
    rows = blocks * cores * block
    out = [
        ((width_t, rows), BF16),
        ((width_s, rows), BF16),
        ((texts, rows), F32),
        ((texts, rows), F32),
        ((width_s, texts), BF16),
        ((8, rows), F32),
    ]
    n = own.shape[0]
    return call(
        first_kernel,
        [(VMEM, own), (pltpu.HBM, image_t), (pltpu.HBM, image_s)],
        out,
        12,
        flops=2 * n * rows * (width_t + width_s),
        size=2 * rows * (width_t + width_s),
        exps=2 * n * rows,
        scratch_shapes=[
            pltpu.VMEM((2 * cores, blocks // 2, block, width_t), BF16),
            pltpu.VMEM((2 * cores, blocks // 2, block, width_s), BF16),
            pltpu.SemaphoreType.DMA((2 * cores, 2)),
        ],
    )


def more_kernel(places, last, *refs):
    count = len(places)
    texts = refs[:count]
    image_t, image_s, _, _, _, before, logit_t, logit_s, turned, stats, joined = refs[count:]
    width_t, rows = image_t.shape
    spans = []
    row = 0
    for at, ref in zip(places, texts):
        n = ref.shape[0]
        spans.append((at, n))
        joined[row : row + n, :] = ref[...]
        turned[:, at : at + n] = ref[:, width_t:].T
        row += n
    for begin in range(0, rows, WIDE):
        cols = slice(begin, begin + WIDE)
        top_t, sum_t, top_s, sum_s, gap = values = tile_logits(
            joined, spans, image_t, image_s, logit_t, logit_s, before, cols
        )
        if not last:
            put_running(stats, cols, values)
            continue
        found = (top_t + jnp.log2(sum_t), top_s + jnp.log2(sum_s), gap / sum_t)
        for q, v in enumerate(found):
            for j in range(WIDE // LANES):
                row = q * (rows // LANES) + begin // LANES + j
                stats[row : row + 1, :] = v[:, j * LANES : j * LANES + LANES]


def more_logits(chunks, state, last=False):
    places = tuple(at for at, _ in chunks)
    image_t, image_s, logit_t, logit_s, turned, stats = state
    width_t, rows = image_t.shape
    width_s = image_s.shape[0]
    n = sum(v.shape[0] for _, v in chunks)
    count = len(chunks)
    shape = ((3 * rows // LANES, LANES), F32) if last else (stats.shape, F32)
    logit_t, logit_s, turned, stats = call(
        functools.partial(more_kernel, places, last),
        [(VMEM, v) for _, v in chunks] + [(VMEM, v) for v in state],
        [(logit_t.shape, F32), (logit_s.shape, F32), (turned.shape, BF16), shape],
        6,
        flops=2 * n * rows * (width_t + width_s),
        size=2 * n * rows,
        exps=2 * n * rows,
        input_output_aliases={count + 2: 0, count + 3: 1, count + 4: 2},
        scratch_shapes=[pltpu.VMEM((n, width_t + width_s), BF16)],
    )
    return image_t, image_s, logit_t, logit_s, turned, stats


def merged(parts):
    def total(v):
        return (v[0] + v[1]) + (v[2] + v[3])

    rows = parts[0].shape[0] // 3
    lse_t, lse_s, gap = ([p[rows * k : rows * k + rows, :] for p in parts] for k in range(3))
    top_t = functools.reduce(jnp.maximum, lse_t)
    top_s = functools.reduce(jnp.maximum, lse_s)
    part_t = [jnp.exp2(v - top_t) for v in lse_t]
    sum_t = total(part_t)
    mean = total([p * g for p, g in zip(part_t, gap)]) / sum_t
    all_s = top_s + jnp.log2(total([jnp.exp2(v - top_s) for v in lse_s]))
    return top_t + jnp.log2(sum_t), all_s, mean


def merge_kernel(a, b, c, d, _, __, out, *held):
    rows = out.shape[0] // 3
    for k, v in enumerate(merged((a, b, c, d))):
        out[rows * k : rows * k + rows, :] = v


def merge(parts, held):
    out, *held = call(
        merge_kernel,
        [(VMEM, v) for v in (*parts, *held)],
        [(parts[0].shape, F32)] + [(v.shape, F32) for v in held],
        4,
        input_output_aliases={4: 1, 5: 2},
    )
    return out, held


def put_merged(parts, lse, loss):
    rows = lse.shape[0] // 2
    all_t, all_s, mean = merged(parts)
    lse[:rows, :] = all_t
    lse[rows:, :] = all_s
    value = (mean - all_t + all_s) * LN2
    for j in range(rows // 2):
        for c in range(2):
            at = c * (rows // 2) + j
            loss[2 * j + c : 2 * j + c + 1, :] = value[at : at + 1, :]


def delta_kernel(
    scale, logit_t, logit_s, turned, image_s, a, b, c, d, other, own, far, left, right, delta, loss, lse
):
    put_merged((a, b, c, d), lse, loss)
    away = 1 - lax.rem(lax.axis_index("grp"), 2)
    rows = logit_t.shape[1]
    half = rows // 2
    blocks, cores, block, width = image_s.shape
    pieces = WIDE // LANES
    for k, out in ((3, far), (1, left), (2, right), (0, own)):
        n = out.shape[0]
        span = slice(n * k, n * k + n)
        for begin in range(0, rows, WIDE):
            cols = slice(begin, begin + WIDE)
            spots = [begin // LANES + j for j in range(pieces)]
            low_t = jnp.concatenate([lse[j : j + 1, :] for j in spots], axis=1)
            low_s = jnp.concatenate(
                [lse[j + rows // LANES : j + rows // LANES + 1, :] for j in spots], axis=1
            )
            prob_t = jnp.exp2(logit_t[span, cols] - low_t)
            prob_s = jnp.exp2(logit_s[span, cols] - low_s)
            delta[begin // half, span, begin % half : begin % half + WIDE] = (
                (prob_s - prob_t) * scale
            ).astype(BF16)
        total = 0.0
        for core in range(cores):
            total += jnp.dot(
                delta[core, span, :],
                image_s[:, core].reshape(blocks * block, width),
                preferred_element_type=F32,
            )
        out[...] = total.astype(out.dtype)
    for begin in range(0, half, WIDE):
        out = jnp.dot(
            turned[...], delta[away, :, begin : begin + WIDE], preferred_element_type=F32
        ).astype(BF16)
        for j in range(pieces):
            other[begin // LANES + j] = out[:, j * LANES : j * LANES + LANES]


def delta_part(logit_t, logit_s, turned, image_s, stats):
    count, rows = logit_t.shape
    width = turned.shape[0]
    return call(
        functools.partial(delta_kernel, 3.0 / math.sqrt(width)),
        [(VMEM, v) for v in (logit_t, logit_s, turned, image_s, *stats)],
        [((rows // 2 // LANES, width, LANES), BF16)]
        + [((count // 4, width), F32 if k == 0 else BF16) for k in range(4)]
        + [((2, count, rows // 2), BF16), ((rows // LANES, LANES), F32)],
        6,
        flops=3 * count * rows * width,
        size=4 * count * rows,
        exps=2 * count * rows,
        scratch_shapes=[pltpu.VMEM((2 * rows // LANES, LANES), F32)],
    )


def image_kernel(turned, delta, other, *outs):
    spot = lax.axis_index("grp")
    core, y, z = lax.rem(spot, 2), lax.rem(lax.div(spot, 2), 4), lax.div(spot, 8)
    for k, out in zip((2, 1, 3, 0), outs[1:] + outs[:1]):
        places = [(z + flip - 2 * z * flip) * 4 + lax.rem(y + k, 4) for flip in range(2)]
        both = jnp.concatenate(
            [delta[core, :, pl.ds(pl.multiple_of(at * LANES, LANES), LANES)] for at in places],
            axis=1,
        )
        mine = jnp.dot(turned[...], both, preferred_element_type=F32)
        for flip, at in enumerate(places):
            out[flip] = (
                mine[:, flip * LANES : flip * LANES + LANES] + other[at].astype(F32)
            ).astype(out.dtype)


def image_part(turned, delta, other):
    _, count, rows = delta.shape
    blocks, width, block = other.shape
    return call(
        image_kernel,
        [(VMEM, turned), (VMEM, delta), (VMEM, other)],
        [((2, width, block), F32 if k == 0 else BF16) for k in range(blocks // 2)],
        4,
        flops=2 * count * rows * width,
        size=count * rows,
    )


def total(parts):
    return functools.reduce(jnp.add, [p.astype(F32) for p in parts])


def shards(image_t, text_t, image_s, text_s):
    width_t, width_s = image_t.shape[1], image_s.shape[1]
    n = text_t.shape[0]
    image_t = image_t.reshape(8, 2, 128, width_t)
    image_s = image_s.reshape(8, 2, 128, width_s)

    own = join(text_t, text_s)
    left = permute(own, along_x(1))
    right = permute(own, along_x(3))
    far = permute(own, along_x(2))
    across = permute(own, cross_z)
    state = first_logits(own, image_t, image_s, 8 * n)
    across, far, running = lax.optimization_barrier((across, far, state[5]))
    state = (*state[:5], running)
    across_left = permute(across, along_x(1))
    across_right = permute(across, along_x(3))
    across_far = permute(far, cross_z)
    state = more_logits([(n, across), (6 * n, far), (2 * n, left), (4 * n, right)], state)
    state = more_logits([(7 * n, across_far)], state)
    state = more_logits([(3 * n, across_left), (5 * n, across_right)], state, last=True)
    _, _, logit_t, logit_s, turned, stats = state
    stats, (logit_t, logit_s) = merge(
        [stats] + [permute(stats, m) for m in (other_core, along_y(0, 1), other_core_and_z)],
        [logit_t, logit_s],
    )
    stats = [stats] + [permute(stats, along_y(k)) for k in (2, 1, 3)]
    grad_other, kept_text, away_far, away_left, away_right, delta, row_loss = delta_part(
        logit_t, logit_s, turned, image_s, stats
    )
    from_core = permute(grad_other, other_core)
    from_far = permute(away_far, along_x(2))
    kept_image, *away_image = image_part(turned, delta, from_core)
    away_left, away_right, _ = lax.optimization_barrier((away_left, away_right, away_image[0]))
    image_terms = [permute(v, along_y(k)) for v, k in zip(away_image, (2, 1, 3))]
    *image_terms, from_far = lax.optimization_barrier((*image_terms, from_far))
    image_sum = total([kept_image] + image_terms)
    text_terms = [kept_text, from_far, permute(away_left, along_x(3)), permute(away_right, along_x(1))]
    from_z = permute(image_sum[1].astype(BF16), along_y(0, 1))
    grad_image = (image_sum[0] + from_z.astype(F32)).T.astype(BF16)
    text_sum = total(text_terms)
    from_across = permute(text_sum[n:].astype(BF16), cross_z)
    grad_text = (text_sum[:n] + from_across.astype(F32)).astype(BF16)
    return row_loss.reshape(-1), grad_image, grad_text


def solution(mesh):
    in_specs = (P("blk", None), P(AXES, None), P("blk", None), P(AXES, None))
    out_specs = (P("blk"), P(AXES, None), P(AXES, None))
    return jax.shard_map(shards, mesh=mesh, in_specs=in_specs, out_specs=out_specs, check_vma=False)
```

```python
import functools
import math

import jax
import jax.numpy as jnp
from jax import lax
from jax.experimental import pallas as pl
from jax.experimental.pallas import tpu as pltpu
from jax.sharding import PartitionSpec as P

AXES = ("blk", "grp")
LOG2E = 1.0 / math.log(2.0)
LN2 = math.log(2.0)
MIB = 1024 * 1024
F32 = jnp.float32
BF16 = jnp.bfloat16
VMEM = pltpu.VMEM
LANES = 128
WIDE = 512


def place(i):
    b, g = divmod(i, 16)
    zh, x = divmod(b, 4)
    zl, r = divmod(g, 8)
    y, c = divmod(r, 2)
    return zh, x, zl, y, c


def index(zh, x, zl, y, c):
    return (zh * 4 + x) * 16 + (zl * 4 + y) * 2 + c


def permute(v, move):
    return lax.ppermute(v, AXES, [(i, index(*move(*place(i)))) for i in range(128)])


def along_x(k):
    return lambda zh, x, zl, y, c: (zh, (x + k) % 4, zl, y, c)


def along_y(k, flip=0):
    return lambda zh, x, zl, y, c: (zh, x, zl ^ flip, (y + k) % 4, c)


def other_core(zh, x, zl, y, c):
    return (zh, x, zl, y, 1 - c)


def cross_z(zh, x, zl, y, c):
    return (1 - zh, x, 1 - zl, y, c)


def call(body, args, out_shape, limit, flops=0, size=0, exps=0, **more):
    specs = [pl.BlockSpec(memory_space=space) for space, _ in args]
    values = [
        v if space is pltpu.SMEM else pltpu.with_memory_space_constraint(v, space)
        for space, v in args
    ]
    return pl.pallas_call(
        body,
        in_specs=specs,
        out_specs=[pl.BlockSpec(memory_space=VMEM)] * len(out_shape),
        out_shape=[VMEM(*s) for s in out_shape],
        compiler_params=pltpu.CompilerParams(vmem_limit_bytes=limit * MIB),
        cost_estimate=pl.CostEstimate(flops=flops, bytes_accessed=size, transcendentals=exps),
        **more,
    )(*values)


def join_kernel(text_t, text_s, out, sems):
    width = text_t.shape[1]
    copies = [
        pltpu.make_async_copy(text_t, out.at[:, :width], sems.at[0]),
        pltpu.make_async_copy(text_s, out.at[:, width:], sems.at[1]),
    ]
    for copy in copies:
        copy.start()
    for copy in copies:
        copy.wait()


def join(text_t, text_s):
    n, width = text_t.shape[0], text_t.shape[1] + text_s.shape[1]
    return call(
        join_kernel,
        [(pltpu.HBM, text_t), (pltpu.HBM, text_s)],
        [((n, width), BF16)],
        4,
        scratch_shapes=[pltpu.SemaphoreType.DMA((2,))],
    )[0]


def scales(width_t, width_s):
    return 3.0 / math.sqrt(width_t) * LOG2E, 3.0 / math.sqrt(width_s) * LOG2E


def tile_logits(text, spans, image_t, image_s, logit_t, logit_s, before, cols):
    width_t = image_t.shape[0]
    scale_t, scale_s = scales(width_t, image_s.shape[0])
    t = jnp.dot(text[:, :width_t], image_t[:, cols], preferred_element_type=F32) * scale_t
    s = jnp.dot(text[:, width_t:], image_s[:, cols], preferred_element_type=F32) * scale_s
    row = 0
    for at, n in spans:
        logit_t[at : at + n, cols] = t[row : row + n]
        logit_s[at : at + n, cols] = s[row : row + n]
        row += n
    top_t = jnp.max(t, axis=0, keepdims=True)
    top_s = jnp.max(s, axis=0, keepdims=True)
    if before is not None:
        old_t, sum_t, old_s, sum_s, gap = (before[k : k + 1, cols] for k in range(5))
        top_t = jnp.maximum(top_t, old_t)
        top_s = jnp.maximum(top_s, old_s)
    sums = []
    for at, n in spans:
        t = logit_t[at : at + n, cols]
        s = logit_s[at : at + n, cols]
        exp_t = jnp.exp2(t - top_t)
        sums.append(
            [
                jnp.sum(v, axis=0, keepdims=True)
                for v in (exp_t, jnp.exp2(s - top_s), exp_t * (t - s))
            ]
        )
    if before is not None:
        shrink = jnp.exp2(old_t - top_t)
        sums.append([sum_t * shrink, sum_s * jnp.exp2(old_s - top_s), gap * shrink])
    new_t, new_s, new_gap = (functools.reduce(jnp.add, v) for v in zip(*sums))
    return top_t, new_t, top_s, new_s, new_gap


def put_running(stats, cols, values):
    for k, v in enumerate(values):
        stats[k : k + 1, cols] = v
    stats[5:8, cols] = jnp.zeros((3, values[0].shape[1]), F32)


def first_kernel(
    own, far_t, far_s, image_t, image_s, logit_t, logit_s, turned, stats, held_t, held_s, sems
):
    blocks, cores, block, width_t = far_t.shape
    width_s = far_s.shape[3]
    half = blocks // 2
    wide = half * block
    copies = []
    for k in range(2 * cores):
        c, j = divmod(k, 2)
        pieces = [
            pltpu.make_async_copy(far_t.at[half * j : half * j + half, c], held_t.at[k], sems.at[k, 0]),
            pltpu.make_async_copy(far_s.at[half * j : half * j + half, c], held_s.at[k], sems.at[k, 1]),
        ]
        for piece in pieces:
            piece.start()
        copies.append(pieces)
    turned[:, : own.shape[0]] = own[:, width_t:].T
    for k, pieces in enumerate(copies):
        for piece in pieces:
            piece.wait()
        cols = slice(k * wide, k * wide + wide)
        image_t[:, cols] = held_t[k].reshape(wide, width_t).T
        image_s[:, cols] = held_s[k].reshape(wide, width_s).T
        spans = [(0, own.shape[0])]
        put_running(
            stats, cols, tile_logits(own, spans, image_t, image_s, logit_t, logit_s, None, cols)
        )


def first_logits(own, image_t, image_s, texts):
    blocks, cores, block, width_t = image_t.shape
    width_s = image_s.shape[3]
    rows = blocks * cores * block
    out = [
        ((width_t, rows), BF16),
        ((width_s, rows), BF16),
        ((texts, rows), F32),
        ((texts, rows), F32),
        ((width_s, texts), BF16),
        ((8, rows), F32),
    ]
    n = own.shape[0]
    return call(
        first_kernel,
        [(VMEM, own), (pltpu.HBM, image_t), (pltpu.HBM, image_s)],
        out,
        12,
        flops=2 * n * rows * (width_t + width_s),
        size=2 * rows * (width_t + width_s),
        exps=2 * n * rows,
        scratch_shapes=[
            pltpu.VMEM((2 * cores, blocks // 2, block, width_t), BF16),
            pltpu.VMEM((2 * cores, blocks // 2, block, width_s), BF16),
            pltpu.SemaphoreType.DMA((2 * cores, 2)),
        ],
    )


def more_kernel(places, last, *refs):
    count = len(places)
    texts = refs[:count]
    image_t, image_s, _, _, _, before, logit_t, logit_s, turned, stats, joined = refs[count:]
    width_t, rows = image_t.shape
    spans = []
    row = 0
    for at, ref in zip(places, texts):
        n = ref.shape[0]
        spans.append((at, n))
        joined[row : row + n, :] = ref[...]
        turned[:, at : at + n] = ref[:, width_t:].T
        row += n
    for begin in range(0, rows, WIDE):
        cols = slice(begin, begin + WIDE)
        top_t, sum_t, top_s, sum_s, gap = values = tile_logits(
            joined, spans, image_t, image_s, logit_t, logit_s, before, cols
        )
        if not last:
            put_running(stats, cols, values)
            continue
        found = (top_t + jnp.log2(sum_t), top_s + jnp.log2(sum_s), gap / sum_t)
        for q, v in enumerate(found):
            for j in range(WIDE // LANES):
                row = q * (rows // LANES) + begin // LANES + j
                stats[row : row + 1, :] = v[:, j * LANES : j * LANES + LANES]


def more_logits(chunks, state, last=False):
    places = tuple(at for at, _ in chunks)
    image_t, image_s, logit_t, logit_s, turned, stats = state
    width_t, rows = image_t.shape
    width_s = image_s.shape[0]
    n = sum(v.shape[0] for _, v in chunks)
    count = len(chunks)
    shape = ((3 * rows // LANES, LANES), F32) if last else (stats.shape, F32)
    logit_t, logit_s, turned, stats = call(
        functools.partial(more_kernel, places, last),
        [(VMEM, v) for _, v in chunks] + [(VMEM, v) for v in state],
        [(logit_t.shape, F32), (logit_s.shape, F32), (turned.shape, BF16), shape],
        6,
        flops=2 * n * rows * (width_t + width_s),
        size=2 * n * rows,
        exps=2 * n * rows,
        input_output_aliases={count + 2: 0, count + 3: 1, count + 4: 2},
        scratch_shapes=[pltpu.VMEM((n, width_t + width_s), BF16)],
    )
    return image_t, image_s, logit_t, logit_s, turned, stats


def merged(parts):
    rows = parts[0].shape[0] // 3
    lse_t, lse_s, gap = ([p[rows * k : rows * k + rows, :] for p in parts] for k in range(3))
    top_t = functools.reduce(jnp.maximum, lse_t)
    top_s = functools.reduce(jnp.maximum, lse_s)
    part_t = [jnp.exp2(v - top_t) for v in lse_t]
    sum_t = functools.reduce(jnp.add, part_t)
    mean = functools.reduce(jnp.add, [p * g for p, g in zip(part_t, gap)]) / sum_t
    sum_s = functools.reduce(jnp.add, [jnp.exp2(v - top_s) for v in lse_s])
    return top_t + jnp.log2(sum_t), top_s + jnp.log2(sum_s), mean


def merge_kernel(mine, other, _, __, out, *held):
    rows = out.shape[1] // 3
    for k, v in enumerate(merged((mine, other))):
        for peer in range(out.shape[0]):
            out[peer, rows * k : rows * k + rows, :] = v


def merge(mine, other, held, copies):
    out, *held = call(
        merge_kernel,
        [(VMEM, v) for v in (mine, other, *held)],
        [((copies, *mine.shape), F32)] + [(v.shape, F32) for v in held],
        4,
        input_output_aliases={2: 1, 3: 2},
    )
    return out, held


def put_merged(received, lse, loss):
    rows = lse.shape[0] // 2
    all_t, all_s, mean = merged([received.at[p] for p in range(received.shape[0])])
    lse[:rows, :] = all_t
    lse[rows:, :] = all_s
    value = (mean - all_t + all_s) * LN2
    for j in range(rows // 2):
        for c in range(2):
            at = c * (rows // 2) + j
            loss[2 * j + c : 2 * j + c + 1, :] = value[at : at + 1, :]


def tile_delta(logit_t, logit_s, lse, scale, begins):
    count, rows = logit_t.shape
    lows, parts = [], []
    for values, first in ((logit_t, 0), (logit_s, rows // LANES)):
        lows.append(
            jnp.concatenate([lse[pl.ds(first + at, 1), :] for at in begins], axis=1)
        )
        parts.append(
            jnp.concatenate(
                [values[:, pl.ds(pl.multiple_of(at * LANES, LANES), LANES)] for at in begins], axis=1
            )
        )
    prob_t, prob_s = (jnp.exp2(part - low) for part, low in zip(parts, lows))
    return ((prob_s - prob_t) * scale).astype(BF16)


PAIR = 2


def away_kernel(scale, logit_t, logit_s, turned, received, out, delta, lse, loss, *held):
    put_merged(received, lse, loss)
    away = 1 - lax.rem(lax.axis_index("grp"), 2)
    blocks = out.shape[0]
    for j in range(0, blocks, PAIR):
        cols = slice(j * LANES, (j + PAIR) * LANES)
        delta[:, cols] = tile_delta(
            logit_t, logit_s, lse, scale, [away * blocks + j + k for k in range(PAIR)]
        )
        grad = jnp.dot(turned[...], delta[:, cols], preferred_element_type=F32).astype(BF16)
        for k in range(PAIR):
            out[j + k] = grad[:, k * LANES : k * LANES + LANES]


def away_part(logit_t, logit_s, turned, received):
    count, rows = logit_t.shape
    width = turned.shape[0]
    return call(
        functools.partial(away_kernel, 3.0 / math.sqrt(width)),
        [(VMEM, v) for v in (logit_t, logit_s, turned, received)],
        [
            ((rows // 2 // LANES, width, LANES), BF16),
            ((count, rows // 2), BF16),
            ((2 * rows // LANES, LANES), F32),
            ((rows // LANES, LANES), F32),
            (logit_t.shape, F32),
            (logit_s.shape, F32),
        ],
        6,
        flops=count * rows * width,
        size=4 * count * rows,
        exps=count * rows,
        input_output_aliases={0: 4, 1: 5},
    )


def near_kernel(scale, logit_t, logit_s, lse, away, image_s, near, *texts):
    core = lax.rem(lax.axis_index("grp"), 2)
    blocks, _, block, width = image_s.shape
    rows = blocks * block
    for j in range(0, blocks, PAIR):
        near[:, j * LANES : (j + PAIR) * LANES] = tile_delta(
            logit_t, logit_s, lse, scale, [core * blocks + j + k for k in range(PAIR)]
        )
    image_near = image_s[:, pl.ds(core, 1)].reshape(rows, width)
    image_away = image_s[:, pl.ds(1 - core, 1)].reshape(rows, width)
    row = 0
    for out in texts:
        span = slice(row, row + out.shape[0])
        row += out.shape[0]
        out[...] = (
            jnp.dot(away[span, :], image_away, preferred_element_type=F32)
            + jnp.dot(near[span, :], image_near, preferred_element_type=F32)
        ).astype(out.dtype)


def near_part(logit_t, logit_s, lse, away, image_s):
    count, rows = logit_t.shape
    width = image_s.shape[3]
    return call(
        functools.partial(near_kernel, 3.0 / math.sqrt(width)),
        [(VMEM, v) for v in (logit_t, logit_s, lse, away, image_s)],
        [(away.shape, BF16)]
        + [
            ((count // part, width), kind)
            for part, kind in ((4, F32), (4, BF16), (4, BF16), (8, F32), (8, BF16))
        ],
        10,
        flops=2 * count * rows * width,
        size=4 * count * rows,
        exps=count * rows,
    )


def image_kernel(turned, near, other, kept, up, down, far, far_flip):
    spot = lax.axis_index("grp")
    y, z = lax.rem(lax.div(spot, 2), 4), lax.div(spot, 8)
    outs = (
        (1, (up.at[0], up.at[1])),
        (3, (down.at[0], down.at[1])),
        (2, (far, far_flip)),
        (0, (kept.at[0], kept.at[1])),
    )
    for k, pair in outs:
        places = [(z + flip - 2 * z * flip) * 4 + lax.rem(y + k, 4) for flip in range(2)]
        both = jnp.concatenate(
            [near[:, pl.ds(pl.multiple_of(at * LANES, LANES), LANES)] for at in places], axis=1
        )
        mine = jnp.dot(turned[...], both, preferred_element_type=F32)
        for flip, (at, out) in enumerate(zip(places, pair)):
            out[...] = (
                mine[:, flip * LANES : flip * LANES + LANES] + other[at].astype(F32)
            ).astype(out.dtype)


def image_part(turned, near, other):
    count, rows = near.shape
    width = turned.shape[0]
    return call(
        image_kernel,
        [(VMEM, turned), (VMEM, near), (VMEM, other)],
        [
            ((2, width, LANES), F32),
            ((2, width, LANES), BF16),
            ((2, width, LANES), BF16),
            ((width, LANES), F32),
            ((width, LANES), BF16),
        ],
        4,
        flops=2 * count * rows * width,
        size=2 * count * rows,
    )


def total(parts):
    return functools.reduce(jnp.add, [p.astype(F32) for p in parts])


def shards(image_t, text_t, image_s, text_s):
    width_t, width_s = image_t.shape[1], image_s.shape[1]
    n = text_t.shape[0]
    image_t = image_t.reshape(8, 2, 128, width_t)
    image_s = image_s.reshape(8, 2, 128, width_s)

    own = join(text_t, text_s)
    left = permute(own, along_x(1))
    right = permute(own, along_x(3))
    far = permute(own, along_x(2))
    across = permute(own, cross_z)
    state = first_logits(own, image_t, image_s, 8 * n)
    across, far, running = lax.optimization_barrier((across, far, state[5]))
    state = (*state[:5], running)
    across_left = permute(across, along_x(1))
    across_right = permute(across, along_x(3))
    across_far = permute(far, cross_z)
    state = more_logits([(n, across), (6 * n, far), (2 * n, left), (4 * n, right)], state)
    state = more_logits([(7 * n, across_far)], state)
    state = more_logits([(3 * n, across_left), (5 * n, across_right)], state, last=True)
    _, _, logit_t, logit_s, turned, stats = state
    stats, (logit_t, logit_s) = merge(stats, permute(stats, other_core), [logit_t, logit_s], 8)
    peers = [[2 * j + c for j in range(8)] for c in range(2)]
    received = lax.all_to_all(stats, "grp", 0, 0, tiled=True, axis_index_groups=peers)
    grad_other, away, lse, row_loss, logit_t, logit_s = away_part(
        logit_t, logit_s, turned, received
    )
    from_core = permute(grad_other, other_core)
    near, *texts = near_part(logit_t, logit_s, lse, away, image_s)
    image_kept, image_up, image_down, image_far, far_flip = image_part(turned, near, from_core)
    from_flip = permute(far_flip, along_y(0, 1))
    from_down, from_up = permute(image_up, along_y(1)), permute(image_down, along_y(3))
    text_kept, text_left, text_right, text_far, far_cross = texts
    far_cross, image_kept = lax.optimization_barrier((far_cross, image_kept))
    from_cross = permute(far_cross, cross_z)
    from_right, from_left = permute(text_left, along_x(3)), permute(text_right, along_x(1))
    image_far = permute((image_far + from_flip.astype(F32)).astype(BF16), along_y(2))
    text_far = permute((text_far + from_cross.astype(F32)).astype(BF16), along_x(2))
    row_loss, from_down = lax.optimization_barrier((row_loss, from_down))
    image_sum = total([image_kept, from_down, from_up])
    text_sum = total([text_kept, from_left, from_right])
    image_sum, text_sum = lax.optimization_barrier((image_sum, text_sum))
    from_z = permute(image_sum[1].astype(BF16), along_y(0, 1))
    from_across = permute(text_sum[n:].astype(BF16), cross_z)
    grad_image = total([image_sum[0], image_far, from_z]).T.astype(BF16)
    grad_text = total([text_sum[:n], text_far, from_across]).astype(BF16)
    return row_loss.reshape(-1), grad_image, grad_text


def solution(mesh):
    in_specs = (P("blk", None), P(AXES, None), P("blk", None), P(AXES, None))
    out_specs = (P("blk"), P(AXES, None), P(AXES, None))
    return jax.shard_map(shards, mesh=mesh, in_specs=in_specs, out_specs=out_specs, check_vma=False)
```

```python
import functools
import math

import jax
import jax.numpy as jnp
from jax import lax
from jax.experimental import pallas as pl
from jax.experimental.pallas import tpu as pltpu
from jax.sharding import PartitionSpec as P

AXES = ("blk", "grp")
LOG2E = 1.0 / math.log(2.0)
LN2 = math.log(2.0)
MIB = 1024 * 1024
F32 = jnp.float32
BF16 = jnp.bfloat16
VMEM = pltpu.VMEM
LANES = 128
WIDE = 512


def place(i):
    b, g = divmod(i, 16)
    zh, x = divmod(b, 4)
    zl, r = divmod(g, 8)
    y, c = divmod(r, 2)
    return zh, x, zl, y, c


def index(zh, x, zl, y, c):
    return (zh * 4 + x) * 16 + (zl * 4 + y) * 2 + c


def permute(v, move):
    return lax.ppermute(v, AXES, [(i, index(*move(*place(i)))) for i in range(128)])


def along_x(k):
    return lambda zh, x, zl, y, c: (zh, (x + k) % 4, zl, y, c)


def along_y(k, flip=0):
    return lambda zh, x, zl, y, c: (zh, x, zl ^ flip, (y + k) % 4, c)


def other_core(zh, x, zl, y, c):
    return (zh, x, zl, y, 1 - c)


def cross_z(zh, x, zl, y, c):
    return (1 - zh, x, 1 - zl, y, c)


def call(body, args, out_shape, limit, flops=0, size=0, exps=0, **more):
    specs = [pl.BlockSpec(memory_space=space) for space, _ in args]
    values = [
        v if space is pltpu.SMEM else pltpu.with_memory_space_constraint(v, space)
        for space, v in args
    ]
    return pl.pallas_call(
        body,
        in_specs=specs,
        out_specs=[
            pl.BlockSpec(memory_space=VMEM if isinstance(s, tuple) else pltpu.HBM) for s in out_shape
        ],
        out_shape=[VMEM(*s) if isinstance(s, tuple) else s for s in out_shape],
        compiler_params=pltpu.CompilerParams(vmem_limit_bytes=limit * MIB),
        cost_estimate=pl.CostEstimate(flops=flops, bytes_accessed=size, transcendentals=exps),
        **more,
    )(*values)


def join_kernel(text_t, text_s, out, sems):
    width = text_t.shape[1]
    copies = [
        pltpu.make_async_copy(text_t, out.at[:, :width], sems.at[0]),
        pltpu.make_async_copy(text_s, out.at[:, width:], sems.at[1]),
    ]
    for copy in copies:
        copy.start()
    for copy in copies:
        copy.wait()


def join(text_t, text_s):
    n, width = text_t.shape[0], text_t.shape[1] + text_s.shape[1]
    return call(
        join_kernel,
        [(pltpu.HBM, text_t), (pltpu.HBM, text_s)],
        [((n, width), BF16)],
        4,
        scratch_shapes=[pltpu.SemaphoreType.DMA((2,))],
    )[0]


def scales(width_t, width_s):
    return 3.0 / math.sqrt(width_t) * LOG2E, 3.0 / math.sqrt(width_s) * LOG2E


def tile_logits(text, spans, image_t, image_s, logit_t, logit_s, before, cols):
    width_t = image_t.shape[0]
    scale_t, scale_s = scales(width_t, image_s.shape[0])
    t = jnp.dot(text[:, :width_t], image_t[:, cols], preferred_element_type=F32) * scale_t
    s = jnp.dot(text[:, width_t:], image_s[:, cols], preferred_element_type=F32) * scale_s
    row = 0
    for at, n in spans:
        logit_t[at : at + n, cols] = t[row : row + n]
        logit_s[at : at + n, cols] = s[row : row + n]
        row += n
    top_t = jnp.max(t, axis=0, keepdims=True)
    top_s = jnp.max(s, axis=0, keepdims=True)
    if before is not None:
        old_t, sum_t, old_s, sum_s, gap = (before[k : k + 1, cols] for k in range(5))
        top_t = jnp.maximum(top_t, old_t)
        top_s = jnp.maximum(top_s, old_s)
    sums = []
    for at, n in spans:
        t = logit_t[at : at + n, cols]
        s = logit_s[at : at + n, cols]
        exp_t = jnp.exp2(t - top_t)
        sums.append(
            [
                jnp.sum(v, axis=0, keepdims=True)
                for v in (exp_t, jnp.exp2(s - top_s), exp_t * (t - s))
            ]
        )
    if before is not None:
        shrink = jnp.exp2(old_t - top_t)
        sums.append([sum_t * shrink, sum_s * jnp.exp2(old_s - top_s), gap * shrink])
    new_t, new_s, new_gap = (functools.reduce(jnp.add, v) for v in zip(*sums))
    return top_t, new_t, top_s, new_s, new_gap


def put_running(stats, cols, values):
    for k, v in enumerate(values):
        stats[k : k + 1, cols] = v
    stats[5:8, cols] = jnp.zeros((3, values[0].shape[1]), F32)


def first_kernel(
    own, far_t, far_s, image_t, image_s, logit_t, logit_s, turned, stats, held_t, held_s, sems
):
    blocks, cores, block, width_t = far_t.shape
    width_s = far_s.shape[3]
    half = blocks // 2
    wide = half * block
    copies = []
    for k in range(2 * cores):
        c, j = divmod(k, 2)
        pieces = [
            pltpu.make_async_copy(far_t.at[half * j : half * j + half, c], held_t.at[k], sems.at[k, 0]),
            pltpu.make_async_copy(far_s.at[half * j : half * j + half, c], held_s.at[k], sems.at[k, 1]),
        ]
        for piece in pieces:
            piece.start()
        copies.append(pieces)
    turned[:, : own.shape[0]] = own[:, width_t:].T
    for k, pieces in enumerate(copies):
        for piece in pieces:
            piece.wait()
        cols = slice(k * wide, k * wide + wide)
        image_t[:, cols] = held_t[k].reshape(wide, width_t).T
        image_s[:, cols] = held_s[k].reshape(wide, width_s).T
        spans = [(0, own.shape[0])]
        put_running(
            stats, cols, tile_logits(own, spans, image_t, image_s, logit_t, logit_s, None, cols)
        )


def first_logits(own, image_t, image_s, texts):
    blocks, cores, block, width_t = image_t.shape
    width_s = image_s.shape[3]
    rows = blocks * cores * block
    out = [
        ((width_t, rows), BF16),
        ((width_s, rows), BF16),
        ((texts, rows), F32),
        ((texts, rows), F32),
        ((width_s, texts), BF16),
        ((8, rows), F32),
    ]
    n = own.shape[0]
    return call(
        first_kernel,
        [(VMEM, own), (pltpu.HBM, image_t), (pltpu.HBM, image_s)],
        out,
        12,
        flops=2 * n * rows * (width_t + width_s),
        size=2 * rows * (width_t + width_s),
        exps=2 * n * rows,
        scratch_shapes=[
            pltpu.VMEM((2 * cores, blocks // 2, block, width_t), BF16),
            pltpu.VMEM((2 * cores, blocks // 2, block, width_s), BF16),
            pltpu.SemaphoreType.DMA((2 * cores, 2)),
        ],
    )


def more_kernel(places, last, *refs):
    count = len(places)
    texts = refs[:count]
    image_t, image_s, _, _, _, before, logit_t, logit_s, turned, stats, joined = refs[count:]
    width_t, rows = image_t.shape
    spans = []
    row = 0
    for at, ref in zip(places, texts):
        n = ref.shape[0]
        spans.append((at, n))
        joined[row : row + n, :] = ref[...]
        turned[:, at : at + n] = ref[:, width_t:].T
        row += n
    for begin in range(0, rows, WIDE):
        cols = slice(begin, begin + WIDE)
        top_t, sum_t, top_s, sum_s, gap = values = tile_logits(
            joined, spans, image_t, image_s, logit_t, logit_s, before, cols
        )
        if not last:
            put_running(stats, cols, values)
            continue
        found = (top_t + jnp.log2(sum_t), top_s + jnp.log2(sum_s), gap / sum_t)
        for q, v in enumerate(found):
            for j in range(WIDE // LANES):
                row = q * (rows // LANES) + begin // LANES + j
                stats[row : row + 1, :] = v[:, j * LANES : j * LANES + LANES]


def more_logits(chunks, state, last=False):
    places = tuple(at for at, _ in chunks)
    image_t, image_s, logit_t, logit_s, turned, stats = state
    width_t, rows = image_t.shape
    width_s = image_s.shape[0]
    n = sum(v.shape[0] for _, v in chunks)
    count = len(chunks)
    shape = ((3 * rows // LANES, LANES), F32) if last else (stats.shape, F32)
    logit_t, logit_s, turned, stats = call(
        functools.partial(more_kernel, places, last),
        [(VMEM, v) for _, v in chunks] + [(VMEM, v) for v in state],
        [(logit_t.shape, F32), (logit_s.shape, F32), (turned.shape, BF16), shape],
        6,
        flops=2 * n * rows * (width_t + width_s),
        size=2 * n * rows,
        exps=2 * n * rows,
        input_output_aliases={count + 2: 0, count + 3: 1, count + 4: 2},
        scratch_shapes=[pltpu.VMEM((n, width_t + width_s), BF16)],
    )
    return image_t, image_s, logit_t, logit_s, turned, stats


def merged(parts):
    rows = parts[0].shape[0] // 3
    lse_t, lse_s, gap = ([p[rows * k : rows * k + rows, :] for p in parts] for k in range(3))
    top_t = functools.reduce(jnp.maximum, lse_t)
    top_s = functools.reduce(jnp.maximum, lse_s)
    part_t = [jnp.exp2(v - top_t) for v in lse_t]
    sum_t = functools.reduce(jnp.add, part_t)
    mean = functools.reduce(jnp.add, [p * g for p, g in zip(part_t, gap)]) / sum_t
    sum_s = functools.reduce(jnp.add, [jnp.exp2(v - top_s) for v in lse_s])
    return top_t + jnp.log2(sum_t), top_s + jnp.log2(sum_s), mean


def merge_kernel(mine, other, _, __, out, *held):
    rows = out.shape[1] // 3
    for k, v in enumerate(merged((mine, other))):
        for peer in range(out.shape[0]):
            out[peer, rows * k : rows * k + rows, :] = v


def merge(mine, other, held, copies):
    out, *held = call(
        merge_kernel,
        [(VMEM, v) for v in (mine, other, *held)],
        [((copies, *mine.shape), F32)] + [(v.shape, F32) for v in held],
        4,
        input_output_aliases={2: 1, 3: 2},
    )
    return out, held


def put_merged(received, lse, loss):
    rows = lse.shape[0] // 2
    all_t, all_s, mean = merged([received.at[p] for p in range(received.shape[0])])
    lse[:rows, :] = all_t
    lse[rows:, :] = all_s
    value = (mean - all_t + all_s) * LN2
    for j in range(rows // 2):
        for c in range(2):
            at = c * (rows // 2) + j
            loss[2 * j + c : 2 * j + c + 1, :] = value[at : at + 1, :]


def tile_delta(logit_t, logit_s, lse, scale, begins):
    count, rows = logit_t.shape
    lows, parts = [], []
    for values, first in ((logit_t, 0), (logit_s, rows // LANES)):
        lows.append(
            jnp.concatenate([lse[pl.ds(first + at, 1), :] for at in begins], axis=1)
        )
        parts.append(
            jnp.concatenate(
                [values[:, pl.ds(pl.multiple_of(at * LANES, LANES), LANES)] for at in begins], axis=1
            )
        )
    prob_t, prob_s = (jnp.exp2(part - low) for part, low in zip(parts, lows))
    return ((prob_s - prob_t) * scale).astype(BF16)


PAIR = 2


def away_kernel(scale, logit_t, logit_s, turned, received, out, delta, lse, loss, *held):
    put_merged(received, lse, loss)
    away = 1 - lax.rem(lax.axis_index("grp"), 2)
    blocks = out.shape[0]
    for j in range(0, blocks, PAIR):
        cols = slice(j * LANES, (j + PAIR) * LANES)
        delta[:, cols] = tile_delta(
            logit_t, logit_s, lse, scale, [away * blocks + j + k for k in range(PAIR)]
        )
        grad = jnp.dot(turned[...], delta[:, cols], preferred_element_type=F32).astype(BF16)
        for k in range(PAIR):
            out[j + k] = grad[:, k * LANES : k * LANES + LANES]


def away_part(logit_t, logit_s, turned, received):
    count, rows = logit_t.shape
    width = turned.shape[0]
    return call(
        functools.partial(away_kernel, 3.0 / math.sqrt(width)),
        [(VMEM, v) for v in (logit_t, logit_s, turned, received)],
        [
            ((rows // 2 // LANES, width, LANES), BF16),
            ((count, rows // 2), BF16),
            ((2 * rows // LANES, LANES), F32),
            ((rows // LANES, LANES), F32),
            (logit_t.shape, F32),
            (logit_s.shape, F32),
        ],
        6,
        flops=count * rows * width,
        size=4 * count * rows,
        exps=count * rows,
        input_output_aliases={0: 4, 1: 5},
    )


def near_kernel(scale, logit_t, logit_s, lse, away, image_s, loss, near, *refs):
    texts, out_loss, sem = refs[:-2], refs[-2], refs[-1]
    copy = pltpu.make_async_copy(loss, out_loss, sem)
    copy.start()
    core = lax.rem(lax.axis_index("grp"), 2)
    blocks, _, block, width = image_s.shape
    rows = blocks * block
    for j in range(0, blocks, PAIR):
        near[:, j * LANES : (j + PAIR) * LANES] = tile_delta(
            logit_t, logit_s, lse, scale, [core * blocks + j + k for k in range(PAIR)]
        )
    image_near = image_s[:, pl.ds(core, 1)].reshape(rows, width)
    image_away = image_s[:, pl.ds(1 - core, 1)].reshape(rows, width)
    row = 0
    for out in texts:
        span = slice(row, row + out.shape[0])
        row += out.shape[0]
        out[...] = (
            jnp.dot(away[span, :], image_away, preferred_element_type=F32)
            + jnp.dot(near[span, :], image_near, preferred_element_type=F32)
        ).astype(out.dtype)
    copy.wait()


def near_part(logit_t, logit_s, lse, away, image_s, loss):
    count, rows = logit_t.shape
    width = image_s.shape[3]
    return call(
        functools.partial(near_kernel, 3.0 / math.sqrt(width)),
        [(VMEM, v) for v in (logit_t, logit_s, lse, away, image_s, loss)],
        [(away.shape, BF16)]
        + [
            ((count // part, width), kind)
            for part, kind in ((4, F32), (4, BF16), (4, BF16), (4, BF16))
        ]
        + [jax.ShapeDtypeStruct(loss.shape, F32)],
        10,
        flops=2 * count * rows * width,
        size=4 * count * rows,
        exps=count * rows,
        scratch_shapes=[pltpu.SemaphoreType.DMA(())],
    )


def image_kernel(turned, near, other, kept, up, down, far, far_flip):
    spot = lax.axis_index("grp")
    y, z = lax.rem(lax.div(spot, 2), 4), lax.div(spot, 8)
    outs = (
        (1, (up.at[0], up.at[1])),
        (3, (down.at[0], down.at[1])),
        (2, (far, far_flip)),
        (0, (kept.at[0], kept.at[1])),
    )
    for k, pair in outs:
        places = [(z + flip - 2 * z * flip) * 4 + lax.rem(y + k, 4) for flip in range(2)]
        both = jnp.concatenate(
            [near[:, pl.ds(pl.multiple_of(at * LANES, LANES), LANES)] for at in places], axis=1
        )
        mine = jnp.dot(turned[...], both, preferred_element_type=F32)
        for flip, (at, out) in enumerate(zip(places, pair)):
            out[...] = (
                mine[:, flip * LANES : flip * LANES + LANES] + other[at].astype(F32)
            ).astype(out.dtype)


def image_part(turned, near, other):
    count, rows = near.shape
    width = turned.shape[0]
    return call(
        image_kernel,
        [(VMEM, turned), (VMEM, near), (VMEM, other)],
        [
            ((2, width, LANES), F32),
            ((2, width, LANES), BF16),
            ((2, width, LANES), BF16),
            ((width, LANES), F32),
            ((width, LANES), BF16),
        ],
        4,
        flops=2 * count * rows * width,
        size=2 * count * rows,
    )


def total(parts):
    return functools.reduce(jnp.add, [p.astype(F32) for p in parts])


def shards(image_t, text_t, image_s, text_s):
    width_t, width_s = image_t.shape[1], image_s.shape[1]
    n = text_t.shape[0]
    image_t = image_t.reshape(8, 2, 128, width_t)
    image_s = image_s.reshape(8, 2, 128, width_s)

    own = join(text_t, text_s)
    left = permute(own, along_x(1))
    right = permute(own, along_x(3))
    far = permute(own, along_x(2))
    across = permute(own, cross_z)
    state = first_logits(own, image_t, image_s, 8 * n)
    across, far, running = lax.optimization_barrier((across, far, state[5]))
    state = (*state[:5], running)
    across_left = permute(across, along_x(1))
    across_right = permute(across, along_x(3))
    across_far = permute(far, cross_z)
    state = more_logits([(n, across), (6 * n, far), (2 * n, left), (4 * n, right)], state)
    state = more_logits([(7 * n, across_far)], state)
    state = more_logits([(3 * n, across_left), (5 * n, across_right)], state, last=True)
    _, _, logit_t, logit_s, turned, stats = state
    stats, (logit_t, logit_s) = merge(stats, permute(stats, other_core), [logit_t, logit_s], 8)
    peers = [[2 * j + c for j in range(8)] for c in range(2)]
    received = lax.all_to_all(stats, "grp", 0, 0, tiled=True, axis_index_groups=peers)
    grad_other, away, lse, row_loss, logit_t, logit_s = away_part(
        logit_t, logit_s, turned, received
    )
    from_core = permute(grad_other, other_core)
    near, *texts, row_loss = near_part(logit_t, logit_s, lse, away, image_s, row_loss)
    image_kept, image_up, image_down, image_far, far_flip = image_part(turned, near, from_core)
    from_flip = permute(far_flip, along_y(0, 1))
    from_down, from_up = permute(image_up, along_y(1)), permute(image_down, along_y(3))
    text_kept, text_left, text_right, text_far = texts
    from_right, from_left = permute(text_left, along_x(3)), permute(text_right, along_x(1))
    image_far = permute((image_far + from_flip.astype(F32)).astype(BF16), along_y(2))
    text_far, from_left, from_right, image_kept = lax.optimization_barrier(
        (text_far, from_left, from_right, image_kept)
    )
    from_far = permute(text_far, along_x(2))
    image_sum = total([image_kept, from_down, from_up])
    from_z = permute(image_sum[1].astype(BF16), along_y(0, 1))
    text_sum = total([text_kept, from_left, from_right, from_far])
    from_across = permute(text_sum[n:].astype(BF16), cross_z)
    grad_image = total([image_sum[0], image_far, from_z]).T.astype(BF16)
    grad_text = total([text_sum[:n], from_across]).astype(BF16)
    return row_loss.reshape(-1), grad_image, grad_text


def solution(mesh):
    in_specs = (P("blk", None), P(AXES, None), P("blk", None), P(AXES, None))
    out_specs = (P("blk"), P(AXES, None), P(AXES, None))
    return jax.shard_map(shards, mesh=mesh, in_specs=in_specs, out_specs=out_specs, check_vma=False)
```

```python
import functools
import math

import jax
import jax.numpy as jnp
from jax import lax
from jax.experimental import pallas as pl
from jax.experimental.pallas import tpu as pltpu
from jax.sharding import PartitionSpec as P

AXES = ("blk", "grp")
LOG2E = 1.0 / math.log(2.0)
LN2 = math.log(2.0)
MIB = 1024 * 1024
F32 = jnp.float32
BF16 = jnp.bfloat16
VMEM = pltpu.VMEM
LANES = 128
WIDE = 512


def place(i):
    b, g = divmod(i, 16)
    zh, x = divmod(b, 4)
    zl, r = divmod(g, 8)
    y, c = divmod(r, 2)
    return zh, x, zl, y, c


def index(zh, x, zl, y, c):
    return (zh * 4 + x) * 16 + (zl * 4 + y) * 2 + c


def permute(v, move):
    return lax.ppermute(v, AXES, [(i, index(*move(*place(i)))) for i in range(128)])


def along_x(k):
    return lambda zh, x, zl, y, c: (zh, (x + k) % 4, zl, y, c)


def along_y(k, flip=0):
    return lambda zh, x, zl, y, c: (zh, x, zl ^ flip, (y + k) % 4, c)


def other_core(zh, x, zl, y, c):
    return (zh, x, zl, y, 1 - c)


def cross_z(zh, x, zl, y, c):
    return (1 - zh, x, 1 - zl, y, c)


def call(body, args, out_shape, limit, flops=0, size=0, exps=0, **more):
    specs = [pl.BlockSpec(memory_space=space) for space, _ in args]
    values = [
        v if space is pltpu.SMEM else pltpu.with_memory_space_constraint(v, space)
        for space, v in args
    ]
    return pl.pallas_call(
        body,
        in_specs=specs,
        out_specs=[
            pl.BlockSpec(memory_space=VMEM if isinstance(s, tuple) else pltpu.HBM) for s in out_shape
        ],
        out_shape=[VMEM(*s) if isinstance(s, tuple) else s for s in out_shape],
        compiler_params=pltpu.CompilerParams(vmem_limit_bytes=limit * MIB),
        cost_estimate=pl.CostEstimate(flops=flops, bytes_accessed=size, transcendentals=exps),
        **more,
    )(*values)


def join_kernel(text_t, text_s, out, sems):
    width = text_t.shape[1]
    copies = [
        pltpu.make_async_copy(text_t, out.at[:, :width], sems.at[0]),
        pltpu.make_async_copy(text_s, out.at[:, width:], sems.at[1]),
    ]
    for copy in copies:
        copy.start()
    for copy in copies:
        copy.wait()


def join(text_t, text_s):
    n, width = text_t.shape[0], text_t.shape[1] + text_s.shape[1]
    return call(
        join_kernel,
        [(pltpu.HBM, text_t), (pltpu.HBM, text_s)],
        [((n, width), BF16)],
        4,
        scratch_shapes=[pltpu.SemaphoreType.DMA((2,))],
    )[0]


def scales(width_t, width_s):
    return 3.0 / math.sqrt(width_t) * LOG2E, 3.0 / math.sqrt(width_s) * LOG2E


def tile_logits(text, spans, image_t, image_s, logit_t, logit_s, before, cols):
    width_t = image_t.shape[0]
    scale_t, scale_s = scales(width_t, image_s.shape[0])
    t = jnp.dot(text[:, :width_t], image_t[:, cols], preferred_element_type=F32) * scale_t
    s = jnp.dot(text[:, width_t:], image_s[:, cols], preferred_element_type=F32) * scale_s
    row = 0
    for at, n in spans:
        logit_t[at : at + n, cols] = t[row : row + n]
        logit_s[at : at + n, cols] = s[row : row + n]
        row += n
    top_t = jnp.max(t, axis=0, keepdims=True)
    top_s = jnp.max(s, axis=0, keepdims=True)
    if before is not None:
        old_t, sum_t, old_s, sum_s, gap = (before[k : k + 1, cols] for k in range(5))
        top_t = jnp.maximum(top_t, old_t)
        top_s = jnp.maximum(top_s, old_s)
    sums = []
    for at, n in spans:
        t = logit_t[at : at + n, cols]
        s = logit_s[at : at + n, cols]
        exp_t = jnp.exp2(t - top_t)
        sums.append(
            [
                jnp.sum(v, axis=0, keepdims=True)
                for v in (exp_t, jnp.exp2(s - top_s), exp_t * (t - s))
            ]
        )
    if before is not None:
        shrink = jnp.exp2(old_t - top_t)
        sums.append([sum_t * shrink, sum_s * jnp.exp2(old_s - top_s), gap * shrink])
    new_t, new_s, new_gap = (functools.reduce(jnp.add, v) for v in zip(*sums))
    return top_t, new_t, top_s, new_s, new_gap


def put_running(stats, cols, values):
    for k, v in enumerate(values):
        stats[k : k + 1, cols] = v
    stats[5:8, cols] = jnp.zeros((3, values[0].shape[1]), F32)


def first_kernel(
    own, far_t, far_s, image_t, image_s, logit_t, logit_s, turned, stats, held_t, held_s, sems
):
    blocks, cores, block, width_t = far_t.shape
    width_s = far_s.shape[3]
    half = blocks // 2
    wide = half * block
    copies = []
    for k in range(2 * cores):
        c, j = divmod(k, 2)
        pieces = [
            pltpu.make_async_copy(far_t.at[half * j : half * j + half, c], held_t.at[k], sems.at[k, 0]),
            pltpu.make_async_copy(far_s.at[half * j : half * j + half, c], held_s.at[k], sems.at[k, 1]),
        ]
        for piece in pieces:
            piece.start()
        copies.append(pieces)
    turned[:, : own.shape[0]] = own[:, width_t:].T
    for k, pieces in enumerate(copies):
        for piece in pieces:
            piece.wait()
        cols = slice(k * wide, k * wide + wide)
        image_t[:, cols] = held_t[k].reshape(wide, width_t).T
        image_s[:, cols] = held_s[k].reshape(wide, width_s).T
        spans = [(0, own.shape[0])]
        put_running(
            stats, cols, tile_logits(own, spans, image_t, image_s, logit_t, logit_s, None, cols)
        )


def first_logits(own, image_t, image_s, texts):
    blocks, cores, block, width_t = image_t.shape
    width_s = image_s.shape[3]
    rows = blocks * cores * block
    out = [
        ((width_t, rows), BF16),
        ((width_s, rows), BF16),
        ((texts, rows), F32),
        ((texts, rows), F32),
        ((width_s, texts), BF16),
        ((8, rows), F32),
    ]
    n = own.shape[0]
    return call(
        first_kernel,
        [(VMEM, own), (pltpu.HBM, image_t), (pltpu.HBM, image_s)],
        out,
        12,
        flops=2 * n * rows * (width_t + width_s),
        size=2 * rows * (width_t + width_s),
        exps=2 * n * rows,
        scratch_shapes=[
            pltpu.VMEM((2 * cores, blocks // 2, block, width_t), BF16),
            pltpu.VMEM((2 * cores, blocks // 2, block, width_s), BF16),
            pltpu.SemaphoreType.DMA((2 * cores, 2)),
        ],
    )


def more_kernel(places, last, *refs):
    count = len(places)
    texts = refs[:count]
    image_t, image_s, _, _, _, before, logit_t, logit_s, turned, stats, joined = refs[count:]
    width_t, rows = image_t.shape
    spans = []
    row = 0
    for at, ref in zip(places, texts):
        n = ref.shape[0]
        spans.append((at, n))
        joined[row : row + n, :] = ref[...]
        turned[:, at : at + n] = ref[:, width_t:].T
        row += n
    for begin in range(0, rows, WIDE):
        cols = slice(begin, begin + WIDE)
        top_t, sum_t, top_s, sum_s, gap = values = tile_logits(
            joined, spans, image_t, image_s, logit_t, logit_s, before, cols
        )
        if not last:
            put_running(stats, cols, values)
            continue
        found = (top_t + jnp.log2(sum_t), top_s + jnp.log2(sum_s), gap / sum_t)
        for q, v in enumerate(found):
            for j in range(WIDE // LANES):
                row = q * (rows // LANES) + begin // LANES + j
                stats[row : row + 1, :] = v[:, j * LANES : j * LANES + LANES]


def more_logits(chunks, state, last=False):
    places = tuple(at for at, _ in chunks)
    image_t, image_s, logit_t, logit_s, turned, stats = state
    width_t, rows = image_t.shape
    width_s = image_s.shape[0]
    n = sum(v.shape[0] for _, v in chunks)
    count = len(chunks)
    shape = ((3 * rows // LANES, LANES), F32) if last else (stats.shape, F32)
    logit_t, logit_s, turned, stats = call(
        functools.partial(more_kernel, places, last),
        [(VMEM, v) for _, v in chunks] + [(VMEM, v) for v in state],
        [(logit_t.shape, F32), (logit_s.shape, F32), (turned.shape, BF16), shape],
        6,
        flops=2 * n * rows * (width_t + width_s),
        size=2 * n * rows,
        exps=2 * n * rows,
        input_output_aliases={count + 2: 0, count + 3: 1, count + 4: 2},
        scratch_shapes=[pltpu.VMEM((n, width_t + width_s), BF16)],
    )
    return image_t, image_s, logit_t, logit_s, turned, stats


def merged(parts):
    rows = parts[0].shape[0] // 3
    lse_t, lse_s, gap = ([p[rows * k : rows * k + rows, :] for p in parts] for k in range(3))
    top_t = functools.reduce(jnp.maximum, lse_t)
    top_s = functools.reduce(jnp.maximum, lse_s)
    part_t = [jnp.exp2(v - top_t) for v in lse_t]
    sum_t = functools.reduce(jnp.add, part_t)
    mean = functools.reduce(jnp.add, [p * g for p, g in zip(part_t, gap)]) / sum_t
    sum_s = functools.reduce(jnp.add, [jnp.exp2(v - top_s) for v in lse_s])
    return top_t + jnp.log2(sum_t), top_s + jnp.log2(sum_s), mean


def merge_kernel(mine, other, _, __, out, *held):
    rows = out.shape[1] // 3
    for k, v in enumerate(merged((mine, other))):
        for peer in range(out.shape[0]):
            out[peer, rows * k : rows * k + rows, :] = v


def merge(mine, other, held, copies):
    out, *held = call(
        merge_kernel,
        [(VMEM, v) for v in (mine, other, *held)],
        [((copies, *mine.shape), F32)] + [(v.shape, F32) for v in held],
        4,
        input_output_aliases={2: 1, 3: 2},
    )
    return out, held


def put_merged(received, lse, loss):
    rows = lse.shape[0] // 2
    all_t, all_s, mean = merged([received.at[p] for p in range(received.shape[0])])
    lse[:rows, :] = all_t
    lse[rows:, :] = all_s
    value = (mean - all_t + all_s) * LN2
    for j in range(rows // 2):
        for c in range(2):
            at = c * (rows // 2) + j
            loss[2 * j + c : 2 * j + c + 1, :] = value[at : at + 1, :]


def tile_delta(logit_t, logit_s, lse, scale, begins):
    count, rows = logit_t.shape
    lows, parts = [], []
    for values, first in ((logit_t, 0), (logit_s, rows // LANES)):
        lows.append(
            jnp.concatenate([lse[pl.ds(first + at, 1), :] for at in begins], axis=1)
        )
        parts.append(
            jnp.concatenate(
                [values[:, pl.ds(pl.multiple_of(at * LANES, LANES), LANES)] for at in begins], axis=1
            )
        )
    prob_t, prob_s = (jnp.exp2(part - low) for part, low in zip(parts, lows))
    return ((prob_s - prob_t) * scale).astype(BF16)


PAIR = 2


def away_kernel(scale, logit_t, logit_s, turned, received, out, delta, lse, loss, *held):
    put_merged(received, lse, loss)
    away = 1 - lax.rem(lax.axis_index("grp"), 2)
    blocks = out.shape[0]
    for j in range(0, blocks, PAIR):
        cols = slice(j * LANES, (j + PAIR) * LANES)
        delta[:, cols] = tile_delta(
            logit_t, logit_s, lse, scale, [away * blocks + j + k for k in range(PAIR)]
        )
        grad = jnp.dot(turned[...], delta[:, cols], preferred_element_type=F32).astype(BF16)
        for k in range(PAIR):
            out[j + k] = grad[:, k * LANES : k * LANES + LANES]


def away_part(logit_t, logit_s, turned, received):
    count, rows = logit_t.shape
    width = turned.shape[0]
    return call(
        functools.partial(away_kernel, 3.0 / math.sqrt(width)),
        [(VMEM, v) for v in (logit_t, logit_s, turned, received)],
        [
            ((rows // 2 // LANES, width, LANES), BF16),
            ((count, rows // 2), BF16),
            ((2 * rows // LANES, LANES), F32),
            ((rows // LANES, LANES), F32),
            (logit_t.shape, F32),
            (logit_s.shape, F32),
        ],
        6,
        flops=count * rows * width,
        size=4 * count * rows,
        exps=count * rows,
        input_output_aliases={0: 4, 1: 5},
    )


def near_kernel(scale, logit_t, logit_s, lse, away, image_s, loss, near, *refs):
    texts, out_loss, sem = refs[:-2], refs[-2], refs[-1]
    copy = pltpu.make_async_copy(loss, out_loss, sem)
    copy.start()
    core = lax.rem(lax.axis_index("grp"), 2)
    blocks, _, block, width = image_s.shape
    rows = blocks * block
    for j in range(0, blocks, PAIR):
        near[:, j * LANES : (j + PAIR) * LANES] = tile_delta(
            logit_t, logit_s, lse, scale, [core * blocks + j + k for k in range(PAIR)]
        )
    image_near = image_s[:, pl.ds(core, 1)].reshape(rows, width)
    image_away = image_s[:, pl.ds(1 - core, 1)].reshape(rows, width)
    row = 0
    for out in texts:
        span = slice(row, row + out.shape[0])
        row += out.shape[0]
        out[...] = (
            jnp.dot(away[span, :], image_away, preferred_element_type=F32)
            + jnp.dot(near[span, :], image_near, preferred_element_type=F32)
        ).astype(out.dtype)
    copy.wait()


def near_part(logit_t, logit_s, lse, away, image_s, loss):
    count, rows = logit_t.shape
    width = image_s.shape[3]
    return call(
        functools.partial(near_kernel, 3.0 / math.sqrt(width)),
        [(VMEM, v) for v in (logit_t, logit_s, lse, away, image_s, loss)],
        [(away.shape, BF16)]
        + [
            ((count // part, width), kind)
            for part, kind in ((4, F32), (4, BF16), (4, BF16), (4, BF16))
        ]
        + [jax.ShapeDtypeStruct(loss.shape, F32)],
        10,
        flops=2 * count * rows * width,
        size=4 * count * rows,
        exps=count * rows,
        scratch_shapes=[pltpu.SemaphoreType.DMA(())],
    )


def image_kernel(turned, near, other, kept, up, down, far, far_flip):
    spot = lax.axis_index("grp")
    y, z = lax.rem(lax.div(spot, 2), 4), lax.div(spot, 8)
    outs = (
        (1, (up.at[0], up.at[1])),
        (3, (down.at[0], down.at[1])),
        (2, (far, far_flip)),
        (0, (kept.at[0], kept.at[1])),
    )
    for k, pair in outs:
        places = [(z + flip - 2 * z * flip) * 4 + lax.rem(y + k, 4) for flip in range(2)]
        both = jnp.concatenate(
            [near[:, pl.ds(pl.multiple_of(at * LANES, LANES), LANES)] for at in places], axis=1
        )
        mine = jnp.dot(turned[...], both, preferred_element_type=F32)
        for flip, (at, out) in enumerate(zip(places, pair)):
            out[...] = (
                mine[:, flip * LANES : flip * LANES + LANES] + other[at].astype(F32)
            ).astype(out.dtype)


def image_part(turned, near, other):
    count, rows = near.shape
    width = turned.shape[0]
    return call(
        image_kernel,
        [(VMEM, turned), (VMEM, near), (VMEM, other)],
        [
            ((2, width, LANES), F32),
            ((2, width, LANES), BF16),
            ((2, width, LANES), BF16),
            ((width, LANES), F32),
            ((width, LANES), BF16),
        ],
        4,
        flops=2 * count * rows * width,
        size=2 * count * rows,
    )


def total(parts):
    return functools.reduce(jnp.add, [p.astype(F32) for p in parts])


def shards(image_t, text_t, image_s, text_s):
    width_t, width_s = image_t.shape[1], image_s.shape[1]
    n = text_t.shape[0]
    image_t = image_t.reshape(8, 2, 128, width_t)
    image_s = image_s.reshape(8, 2, 128, width_s)

    own = join(text_t, text_s)
    left = permute(own, along_x(1))
    right = permute(own, along_x(3))
    far = permute(own, along_x(2))
    across = permute(own, cross_z)
    state = first_logits(own, image_t, image_s, 8 * n)
    across, far, running = lax.optimization_barrier((across, far, state[5]))
    state = (*state[:5], running)
    across_left = permute(across, along_x(1))
    across_right = permute(across, along_x(3))
    across_far = permute(far, cross_z)
    state = more_logits([(n, across), (6 * n, far), (2 * n, left), (4 * n, right)], state)
    state = more_logits([(7 * n, across_far)], state)
    state = more_logits([(3 * n, across_left), (5 * n, across_right)], state, last=True)
    _, _, logit_t, logit_s, turned, stats = state
    stats, (logit_t, logit_s) = merge(stats, permute(stats, other_core), [logit_t, logit_s], 8)
    peers = [[2 * j + c for j in range(8)] for c in range(2)]
    received = lax.all_to_all(stats, "grp", 0, 0, tiled=True, axis_index_groups=peers)
    grad_other, away, lse, row_loss, logit_t, logit_s = away_part(
        logit_t, logit_s, turned, received
    )
    from_core = permute(grad_other, other_core)
    near, *texts, row_loss = near_part(logit_t, logit_s, lse, away, image_s, row_loss)
    image_kept, image_up, image_down, image_far, far_flip = image_part(turned, near, from_core)
    from_flip = permute(far_flip, along_y(0, 1))
    from_down, from_up = permute(image_up, along_y(1)), permute(image_down, along_y(3))
    text_kept, text_left, text_right, text_far = texts
    from_far = permute(text_far, along_x(2))
    text_left, text_right, from_far, image_kept = lax.optimization_barrier(
        (text_left, text_right, from_far, image_kept)
    )
    from_right, from_left = permute(text_left, along_x(3)), permute(text_right, along_x(1))
    image_far = permute((image_far + from_flip.astype(F32)).astype(BF16), along_y(2))
    image_sum = total([image_kept, from_down, from_up])
    from_z = permute(image_sum[1].astype(BF16), along_y(0, 1))
    text_sum = total([text_kept, from_left, from_right, from_far])
    from_across = permute(text_sum[n:].astype(BF16), cross_z)
    grad_image = total([image_sum[0], image_far, from_z]).T.astype(BF16)
    grad_text = total([text_sum[:n], from_across]).astype(BF16)
    return row_loss.reshape(-1), grad_image, grad_text


def solution(mesh):
    in_specs = (P("blk", None), P(AXES, None), P("blk", None), P(AXES, None))
    out_specs = (P("blk"), P(AXES, None), P(AXES, None))
    return jax.shard_map(shards, mesh=mesh, in_specs=in_specs, out_specs=out_specs, check_vma=False)
```

```python
import functools
import math

import jax
import jax.numpy as jnp
from jax import lax
from jax.experimental import pallas as pl
from jax.experimental.pallas import tpu as pltpu
from jax.sharding import PartitionSpec as P

AXES = ("blk", "grp")
LOG2E = 1.0 / math.log(2.0)
LN2 = math.log(2.0)
MIB = 1024 * 1024
F32 = jnp.float32
BF16 = jnp.bfloat16
VMEM = pltpu.VMEM
LANES = 128
WIDE = 512


def place(i):
    b, g = divmod(i, 16)
    zh, x = divmod(b, 4)
    zl, r = divmod(g, 8)
    y, c = divmod(r, 2)
    return zh, x, zl, y, c


def index(zh, x, zl, y, c):
    return (zh * 4 + x) * 16 + (zl * 4 + y) * 2 + c


def permute(v, move):
    return lax.ppermute(v, AXES, [(i, index(*move(*place(i)))) for i in range(128)])


def along_x(k):
    return lambda zh, x, zl, y, c: (zh, (x + k) % 4, zl, y, c)


def along_y(k, flip=0):
    return lambda zh, x, zl, y, c: (zh, x, zl ^ flip, (y + k) % 4, c)


def other_core(zh, x, zl, y, c):
    return (zh, x, zl, y, 1 - c)


def cross_z(zh, x, zl, y, c):
    return (1 - zh, x, 1 - zl, y, c)


def call(body, args, out_shape, limit, flops=0, size=0, exps=0, **more):
    specs = [pl.BlockSpec(memory_space=space) for space, _ in args]
    values = [
        v if space is pltpu.SMEM else pltpu.with_memory_space_constraint(v, space)
        for space, v in args
    ]
    return pl.pallas_call(
        body,
        in_specs=specs,
        out_specs=[
            pl.BlockSpec(memory_space=VMEM if isinstance(s, tuple) else pltpu.HBM) for s in out_shape
        ],
        out_shape=[VMEM(*s) if isinstance(s, tuple) else s for s in out_shape],
        compiler_params=pltpu.CompilerParams(vmem_limit_bytes=limit * MIB),
        cost_estimate=pl.CostEstimate(flops=flops, bytes_accessed=size, transcendentals=exps),
        **more,
    )(*values)


def join_kernel(text_t, text_s, out, sems):
    width = text_t.shape[1]
    copies = [
        pltpu.make_async_copy(text_t, out.at[:, :width], sems.at[0]),
        pltpu.make_async_copy(text_s, out.at[:, width:], sems.at[1]),
    ]
    for copy in copies:
        copy.start()
    for copy in copies:
        copy.wait()


def join(text_t, text_s):
    n, width = text_t.shape[0], text_t.shape[1] + text_s.shape[1]
    return call(
        join_kernel,
        [(pltpu.HBM, text_t), (pltpu.HBM, text_s)],
        [((n, width), BF16)],
        4,
        scratch_shapes=[pltpu.SemaphoreType.DMA((2,))],
    )[0]


def scales(width_t, width_s):
    return 3.0 / math.sqrt(width_t) * LOG2E, 3.0 / math.sqrt(width_s) * LOG2E


def tile_logits(text, spans, image_t, image_s, logit_t, logit_s, before, cols):
    width_t = image_t.shape[0]
    scale_t, scale_s = scales(width_t, image_s.shape[0])
    t = jnp.dot(text[:, :width_t], image_t[:, cols], preferred_element_type=F32) * scale_t
    s = jnp.dot(text[:, width_t:], image_s[:, cols], preferred_element_type=F32) * scale_s
    row = 0
    for at, n in spans:
        logit_t[at : at + n, cols] = t[row : row + n]
        logit_s[at : at + n, cols] = s[row : row + n]
        row += n
    top_t = jnp.max(t, axis=0, keepdims=True)
    top_s = jnp.max(s, axis=0, keepdims=True)
    if before is not None:
        old_t, sum_t, old_s, sum_s, gap = (before[k : k + 1, cols] for k in range(5))
        top_t = jnp.maximum(top_t, old_t)
        top_s = jnp.maximum(top_s, old_s)
    sums = []
    for at, n in spans:
        t = logit_t[at : at + n, cols]
        s = logit_s[at : at + n, cols]
        exp_t = jnp.exp2(t - top_t)
        sums.append(
            [
                jnp.sum(v, axis=0, keepdims=True)
                for v in (exp_t, jnp.exp2(s - top_s), exp_t * (t - s))
            ]
        )
    if before is not None:
        shrink = jnp.exp2(old_t - top_t)
        sums.append([sum_t * shrink, sum_s * jnp.exp2(old_s - top_s), gap * shrink])
    new_t, new_s, new_gap = (functools.reduce(jnp.add, v) for v in zip(*sums))
    return top_t, new_t, top_s, new_s, new_gap


def put_running(stats, cols, values):
    for k, v in enumerate(values):
        stats[k : k + 1, cols] = v
    stats[5:8, cols] = jnp.zeros((3, values[0].shape[1]), F32)


def first_kernel(
    own, far_t, far_s, image_t, image_s, logit_t, logit_s, turned, stats, held_t, held_s, sems
):
    blocks, cores, block, width_t = far_t.shape
    width_s = far_s.shape[3]
    half = blocks // 2
    wide = half * block
    copies = []
    for k in range(2 * cores):
        c, j = divmod(k, 2)
        pieces = [
            pltpu.make_async_copy(far_t.at[half * j : half * j + half, c], held_t.at[k], sems.at[k, 0]),
            pltpu.make_async_copy(far_s.at[half * j : half * j + half, c], held_s.at[k], sems.at[k, 1]),
        ]
        for piece in pieces:
            piece.start()
        copies.append(pieces)
    turned[:, : own.shape[0]] = own[:, width_t:].T
    for k, pieces in enumerate(copies):
        for piece in pieces:
            piece.wait()
        cols = slice(k * wide, k * wide + wide)
        image_t[:, cols] = held_t[k].reshape(wide, width_t).T
        image_s[:, cols] = held_s[k].reshape(wide, width_s).T
        spans = [(0, own.shape[0])]
        put_running(
            stats, cols, tile_logits(own, spans, image_t, image_s, logit_t, logit_s, None, cols)
        )


def first_logits(own, image_t, image_s, texts):
    blocks, cores, block, width_t = image_t.shape
    width_s = image_s.shape[3]
    rows = blocks * cores * block
    out = [
        ((width_t, rows), BF16),
        ((width_s, rows), BF16),
        ((texts, rows), F32),
        ((texts, rows), F32),
        ((width_s, texts), BF16),
        ((8, rows), F32),
    ]
    n = own.shape[0]
    return call(
        first_kernel,
        [(VMEM, own), (pltpu.HBM, image_t), (pltpu.HBM, image_s)],
        out,
        12,
        flops=2 * n * rows * (width_t + width_s),
        size=2 * rows * (width_t + width_s),
        exps=2 * n * rows,
        scratch_shapes=[
            pltpu.VMEM((2 * cores, blocks // 2, block, width_t), BF16),
            pltpu.VMEM((2 * cores, blocks // 2, block, width_s), BF16),
            pltpu.SemaphoreType.DMA((2 * cores, 2)),
        ],
    )


def more_kernel(places, last, *refs):
    count = len(places)
    texts = refs[:count]
    image_t, image_s, _, _, _, before, logit_t, logit_s, turned, stats, joined = refs[count:]
    width_t, rows = image_t.shape
    spans = []
    row = 0
    for at, ref in zip(places, texts):
        n = ref.shape[0]
        spans.append((at, n))
        joined[row : row + n, :] = ref[...]
        turned[:, at : at + n] = ref[:, width_t:].T
        row += n
    for begin in range(0, rows, WIDE):
        cols = slice(begin, begin + WIDE)
        top_t, sum_t, top_s, sum_s, gap = values = tile_logits(
            joined, spans, image_t, image_s, logit_t, logit_s, before, cols
        )
        if not last:
            put_running(stats, cols, values)
            continue
        found = (top_t + jnp.log2(sum_t), top_s + jnp.log2(sum_s), gap / sum_t)
        for q, v in enumerate(found):
            for j in range(WIDE // LANES):
                row = q * (rows // LANES) + begin // LANES + j
                stats[row : row + 1, :] = v[:, j * LANES : j * LANES + LANES]


def more_logits(chunks, state, last=False):
    places = tuple(at for at, _ in chunks)
    image_t, image_s, logit_t, logit_s, turned, stats = state
    width_t, rows = image_t.shape
    width_s = image_s.shape[0]
    n = sum(v.shape[0] for _, v in chunks)
    count = len(chunks)
    shape = ((3 * rows // LANES, LANES), F32) if last else (stats.shape, F32)
    logit_t, logit_s, turned, stats = call(
        functools.partial(more_kernel, places, last),
        [(VMEM, v) for _, v in chunks] + [(VMEM, v) for v in state],
        [(logit_t.shape, F32), (logit_s.shape, F32), (turned.shape, BF16), shape],
        6,
        flops=2 * n * rows * (width_t + width_s),
        size=2 * n * rows,
        exps=2 * n * rows,
        input_output_aliases={count + 2: 0, count + 3: 1, count + 4: 2},
        scratch_shapes=[pltpu.VMEM((n, width_t + width_s), BF16)],
    )
    return image_t, image_s, logit_t, logit_s, turned, stats


def merged(parts):
    rows = parts[0].shape[0] // 3
    lse_t, lse_s, gap = ([p[rows * k : rows * k + rows, :] for p in parts] for k in range(3))
    top_t = functools.reduce(jnp.maximum, lse_t)
    top_s = functools.reduce(jnp.maximum, lse_s)
    part_t = [jnp.exp2(v - top_t) for v in lse_t]
    sum_t = functools.reduce(jnp.add, part_t)
    mean = functools.reduce(jnp.add, [p * g for p, g in zip(part_t, gap)]) / sum_t
    sum_s = functools.reduce(jnp.add, [jnp.exp2(v - top_s) for v in lse_s])
    return top_t + jnp.log2(sum_t), top_s + jnp.log2(sum_s), mean


def merge_kernel(mine, other, _, __, out, *held):
    rows = out.shape[1] // 3
    for k, v in enumerate(merged((mine, other))):
        for peer in range(out.shape[0]):
            out[peer, rows * k : rows * k + rows, :] = v


def merge(mine, other, held, copies):
    out, *held = call(
        merge_kernel,
        [(VMEM, v) for v in (mine, other, *held)],
        [((copies, *mine.shape), F32)] + [(v.shape, F32) for v in held],
        4,
        input_output_aliases={2: 1, 3: 2},
    )
    return out, held


def put_merged(received, lse, loss):
    rows = lse.shape[0] // 2
    all_t, all_s, mean = merged([received.at[p] for p in range(received.shape[0])])
    lse[:rows, :] = all_t
    lse[rows:, :] = all_s
    value = (mean - all_t + all_s) * LN2
    for j in range(rows // 2):
        for c in range(2):
            at = c * (rows // 2) + j
            loss[2 * j + c : 2 * j + c + 1, :] = value[at : at + 1, :]


def tile_delta(logit_t, logit_s, lse, scale, begins):
    count, rows = logit_t.shape
    lows, parts = [], []
    for values, first in ((logit_t, 0), (logit_s, rows // LANES)):
        lows.append(
            jnp.concatenate([lse[pl.ds(first + at, 1), :] for at in begins], axis=1)
        )
        parts.append(
            jnp.concatenate(
                [values[:, pl.ds(pl.multiple_of(at * LANES, LANES), LANES)] for at in begins], axis=1
            )
        )
    prob_t, prob_s = (jnp.exp2(part - low) for part, low in zip(parts, lows))
    return ((prob_s - prob_t) * scale).astype(BF16)


PAIR = 2


def away_kernel(scale, logit_t, logit_s, turned, received, out, delta, lse, loss, *held):
    put_merged(received, lse, loss)
    away = 1 - lax.rem(lax.axis_index("grp"), 2)
    blocks = out.shape[0]
    for j in range(0, blocks, PAIR):
        cols = slice(j * LANES, (j + PAIR) * LANES)
        delta[:, cols] = tile_delta(
            logit_t, logit_s, lse, scale, [away * blocks + j + k for k in range(PAIR)]
        )
        grad = jnp.dot(turned[...], delta[:, cols], preferred_element_type=F32).astype(BF16)
        for k in range(PAIR):
            out[j + k] = grad[:, k * LANES : k * LANES + LANES]


def away_part(logit_t, logit_s, turned, received):
    count, rows = logit_t.shape
    width = turned.shape[0]
    return call(
        functools.partial(away_kernel, 3.0 / math.sqrt(width)),
        [(VMEM, v) for v in (logit_t, logit_s, turned, received)],
        [
            ((rows // 2 // LANES, width, LANES), BF16),
            ((count, rows // 2), BF16),
            ((2 * rows // LANES, LANES), F32),
            ((rows // LANES, LANES), F32),
            (logit_t.shape, F32),
            (logit_s.shape, F32),
        ],
        6,
        flops=count * rows * width,
        size=4 * count * rows,
        exps=count * rows,
        input_output_aliases={0: 4, 1: 5},
    )


def near_kernel(scale, logit_t, logit_s, lse, away, image_s, near, *texts):
    core = lax.rem(lax.axis_index("grp"), 2)
    blocks, _, block, width = image_s.shape
    rows = blocks * block
    for j in range(0, blocks, PAIR):
        near[:, j * LANES : (j + PAIR) * LANES] = tile_delta(
            logit_t, logit_s, lse, scale, [core * blocks + j + k for k in range(PAIR)]
        )
    image_near = image_s[:, pl.ds(core, 1)].reshape(rows, width)
    image_away = image_s[:, pl.ds(1 - core, 1)].reshape(rows, width)
    row = 0
    for out in texts:
        span = slice(row, row + out.shape[0])
        row += out.shape[0]
        out[...] = (
            jnp.dot(away[span, :], image_away, preferred_element_type=F32)
            + jnp.dot(near[span, :], image_near, preferred_element_type=F32)
        ).astype(out.dtype)


def near_part(logit_t, logit_s, lse, away, image_s):
    count, rows = logit_t.shape
    width = image_s.shape[3]
    return call(
        functools.partial(near_kernel, 3.0 / math.sqrt(width)),
        [(VMEM, v) for v in (logit_t, logit_s, lse, away, image_s)],
        [(away.shape, BF16)]
        + [
            ((count // part, width), kind)
            for part, kind in ((4, F32), (4, BF16), (4, BF16), (4, BF16))
        ],
        10,
        flops=2 * count * rows * width,
        size=4 * count * rows,
        exps=count * rows,
    )


def image_kernel(turned, near, other, loss, kept, up, down, far, far_flip, out_loss, sem):
    copy = pltpu.make_async_copy(loss, out_loss, sem)
    copy.start()
    spot = lax.axis_index("grp")
    y, z = lax.rem(lax.div(spot, 2), 4), lax.div(spot, 8)
    outs = (
        (1, (up.at[0], up.at[1])),
        (3, (down.at[0], down.at[1])),
        (2, (far, far_flip)),
        (0, (kept.at[0], kept.at[1])),
    )
    for k, pair in outs:
        places = [(z + flip - 2 * z * flip) * 4 + lax.rem(y + k, 4) for flip in range(2)]
        both = jnp.concatenate(
            [near[:, pl.ds(pl.multiple_of(at * LANES, LANES), LANES)] for at in places], axis=1
        )
        mine = jnp.dot(turned[...], both, preferred_element_type=F32)
        for flip, (at, out) in enumerate(zip(places, pair)):
            out[...] = (
                mine[:, flip * LANES : flip * LANES + LANES] + other[at].astype(F32)
            ).astype(out.dtype)
    copy.wait()


def image_part(turned, near, other, loss):
    count, rows = near.shape
    width = turned.shape[0]
    return call(
        image_kernel,
        [(VMEM, turned), (VMEM, near), (VMEM, other), (VMEM, loss)],
        [
            ((2, width, LANES), F32),
            ((2, width, LANES), BF16),
            ((2, width, LANES), BF16),
            ((width, LANES), F32),
            ((width, LANES), BF16),
            jax.ShapeDtypeStruct(loss.shape, F32),
        ],
        4,
        scratch_shapes=[pltpu.SemaphoreType.DMA(())],
        flops=2 * count * rows * width,
        size=2 * count * rows,
    )


def total(parts):
    return functools.reduce(jnp.add, [p.astype(F32) for p in parts])


def shards(image_t, text_t, image_s, text_s):
    width_t, width_s = image_t.shape[1], image_s.shape[1]
    n = text_t.shape[0]
    image_t = image_t.reshape(8, 2, 128, width_t)
    image_s = image_s.reshape(8, 2, 128, width_s)

    own = join(text_t, text_s)
    left = permute(own, along_x(1))
    right = permute(own, along_x(3))
    far = permute(own, along_x(2))
    across = permute(own, cross_z)
    state = first_logits(own, image_t, image_s, 8 * n)
    across, far, running = lax.optimization_barrier((across, far, state[5]))
    state = (*state[:5], running)
    across_left = permute(across, along_x(1))
    across_right = permute(across, along_x(3))
    across_far = permute(far, cross_z)
    state = more_logits([(n, across), (6 * n, far), (2 * n, left), (4 * n, right)], state)
    state = more_logits([(7 * n, across_far)], state)
    state = more_logits([(3 * n, across_left), (5 * n, across_right)], state, last=True)
    _, _, logit_t, logit_s, turned, stats = state
    stats, (logit_t, logit_s) = merge(stats, permute(stats, other_core), [logit_t, logit_s], 8)
    peers = [[2 * j + c for j in range(8)] for c in range(2)]
    received = lax.all_to_all(stats, "grp", 0, 0, tiled=True, axis_index_groups=peers)
    grad_other, away, lse, row_loss, logit_t, logit_s = away_part(
        logit_t, logit_s, turned, received
    )
    from_core = permute(grad_other, other_core)
    near, *texts = near_part(logit_t, logit_s, lse, away, image_s)
    image_kept, image_up, image_down, image_far, far_flip, row_loss = image_part(
        turned, near, from_core, row_loss
    )
    from_flip = permute(far_flip, along_y(0, 1))
    from_down, from_up = permute(image_up, along_y(1)), permute(image_down, along_y(3))
    text_kept, text_left, text_right, text_far = texts
    from_far = permute(text_far, along_x(2))
    text_left, text_right, from_far, image_kept = lax.optimization_barrier(
        (text_left, text_right, from_far, image_kept)
    )
    from_right, from_left = permute(text_left, along_x(3)), permute(text_right, along_x(1))
    image_far = permute((image_far + from_flip.astype(F32)).astype(BF16), along_y(2))
    image_sum = total([image_kept, from_down, from_up])
    from_z = permute(image_sum[1].astype(BF16), along_y(0, 1))
    text_sum = total([text_kept, from_left, from_right, from_far])
    from_across = permute(text_sum[n:].astype(BF16), cross_z)
    grad_image = total([image_sum[0], image_far, from_z]).T.astype(BF16)
    grad_text = total([text_sum[:n], from_across]).astype(BF16)
    return row_loss.reshape(-1), grad_image, grad_text


def solution(mesh):
    in_specs = (P("blk", None), P(AXES, None), P("blk", None), P(AXES, None))
    out_specs = (P("blk"), P(AXES, None), P(AXES, None))
    return jax.shard_map(shards, mesh=mesh, in_specs=in_specs, out_specs=out_specs, check_vma=False)
```
